128 devices in a mesh: freq: 16 (over y, x_lo, core), panel: 8 (over x_hi, z).
Axes of the slice: x: 4 (x_hi: 2, x_lo: 2; x = x_hi * 2 + x_lo), y: 4, z: 4, core: 2. Of those that a mesh axis runs over, the one named last changes fastest.
Arguments:
- reflection: bfloat16 [2, 128, 2048, 2048], P(None, 'freq', None, 'panel'), may hold values from -0.1875 to 0.1875
- focus_init: float32 [512, 48, 2048], P('freq', None, 'panel'), may hold values from -6 to 6
- onsets: int32 [48, 2048], P(None, 'panel'), may hold values from 64 to 191
Outputs:
- focusing: float32 [512, 48, 2048], P('freq', None, 'panel')
- upgoing: float32 [512, 48, 2048], P('freq', None, 'panel')
The draws below stay inside these ranges and needn't reach their ends.
All inputs are finite; a program needn't handle non-finite values.
Results may differ from the reference program's by a relative error of at most 0.023.
Values may be sent and summed in bfloat16 or wider, within the bound.
No kernel may reach another device: no remote copies, remote signals or barrier semaphores. Data moves between devices by JAX's collectives and lax.ppermute only.
A program may use at most 128 MiB of HBM per device.

```python
import math
import jax
import jax.numpy as jnp
from jax import lax

N = 2048
NT = 512
VS = 48
ITERS = 2
NF = 128
N_PANEL = 8


def plant(result, own_key, smallest, largest):
    index_at = [jax.random.randint(jax.random.fold_in(own_key, axis), (), 0, length) for axis, length in enumerate(result.shape)]
    widest = result.shape.index(max(result.shape))
    beside = index_at[:widest] + [(index_at[widest] + 1) % result.shape[widest]] + index_at[widest + 1:]
    return result.at[tuple(index_at)].set(smallest).at[tuple(beside)].set(largest)


def shard_levels(key, extent, shards, least, top_value):
    factor_of, own = 1.0, jax.random.fold_in(key, 6)
    for axis_at, shards_of in shards:
        heights = jnp.exp(jax.random.uniform(jax.random.fold_in(own, axis_at), (shards_of,), jnp.float32, least / len(shards), top_value / len(shards)))
        factor_of = factor_of * jnp.repeat(heights, extent[axis_at] // shards_of).reshape([-1 if axis == axis_at else 1 for axis in range(len(extent))])
    return factor_of


def bell_draw(stream_key, shape, width, most, cuts=(), held_as=jnp.bfloat16):
    values = width * jax.random.normal(stream_key, shape, jnp.float32)
    if cuts:
        values = values * shard_levels(stream_key, shape, cuts, -0.22, 0.18)
    return jnp.clip(values, -most, most).astype(held_as)


def setup_inputs(seed: int = 0) -> dict:
    keys = jax.random.split(jax.random.key(seed), 4)
    return {
        "reflection": bell_draw(keys[0], (2, NF, N, N), (N // 2) ** -0.5, 0.1875, ((1, 16), (3, 8))),
        "focus_init": bell_draw(keys[1], (NT, VS, N), 1.0, 6.0, ((0, 16), (2, 8)), jnp.float32),
        "onsets": plant(jax.random.randint(keys[2], (VS, N), NT // 8, 3 * NT // 8), jax.random.fold_in(keys[2], 1), NT // 8, (3 * NT // 8) - 1).astype(jnp.int32),
    }


def band_tables(freq_count, time_count):
    harmonic = jnp.arange(1, freq_count + 1, dtype=jnp.int32)
    samples = jnp.arange(time_count, dtype=jnp.int32)
    phases = harmonic[:, None] * samples[None, :] % time_count
    angles = phases.astype(jnp.float32) * jnp.float32(2.0 * math.pi / time_count)
    factor = 1.0 / math.sqrt(time_count)
    cosines = jnp.stack([jnp.cos(angles), -jnp.sin(angles)], axis=1).reshape(2 * freq_count, time_count)
    forward = cosines * jnp.float32(factor)
    inverse = jnp.transpose(cosines) * jnp.float32(2.0 * factor)
    return (forward, inverse)

def windowed(traces, onsets):
    samples = jnp.arange(NT, dtype=jnp.int32)[:, None, None]
    kept_mask = (samples < onsets[None]) | (samples > NT - onsets[None])
    return jnp.where(kept_mask, traces, jnp.zeros_like(traces))

def spectra_of(traces, forward):
    spectra = jnp.dot(forward, traces.reshape(NT, VS * N), precision=lax.Precision.HIGHEST, preferred_element_type=jnp.float32)
    return spectra.reshape(NF, 2, VS, N).astype(jnp.bfloat16)

def traces_of(spectra, inverse):
    traces = jnp.dot(inverse, spectra.reshape(2 * NF, VS * N), precision=lax.Precision.HIGHEST, preferred_element_type=jnp.float32)
    return traces.reshape(NT, VS, N)

def image_one(freq_index, reflection, spectra):
    matrix = lax.dynamic_index_in_dim(reflection, freq_index, 1, keepdims=False).astype(jnp.float32)
    source = lax.dynamic_index_in_dim(spectra, freq_index, 0, keepdims=False).astype(jnp.float32)
    blocked = matrix.reshape(2, N, N_PANEL, N // N_PANEL)
    sources = source.reshape(2, VS, N_PANEL, N // N_PANEL)
    products = jnp.einsum('crps,dvps->pcdvr', blocked, sources, precision=lax.Precision.HIGHEST)
    real_part = products[:, 0, 0] - products[:, 1, 1]
    imag_part = products[:, 0, 1] + products[:, 1, 0]
    partial_sums = jnp.stack([real_part, imag_part], axis=1).astype(jnp.bfloat16)
    partial_sums = lax.optimization_barrier(partial_sums)
    return lax.optimization_barrier(jnp.sum(partial_sums.astype(jnp.float32), axis=0))

def return_one(freq_index, reflection, spectra):
    matrix = lax.dynamic_index_in_dim(reflection, freq_index, 1, keepdims=False).astype(jnp.float32)
    upgoing = lax.dynamic_index_in_dim(spectra, freq_index, 0, keepdims=False).astype(jnp.float32)
    products = jnp.einsum('crs,dvr->cdvs', matrix, upgoing, precision=lax.Precision.HIGHEST)
    real_part = products[0, 0] + products[1, 1]
    imag_part = products[0, 1] - products[1, 0]
    return jnp.stack([real_part, imag_part], axis=0)

def reference(reflection, focus_init, onsets):
    forward, inverse = band_tables(NF, NT)
    indices = jnp.arange(NF, dtype=jnp.int32)
    focusing = focus_init
    upgoing = focus_init
    for iteration in range(ITERS):
        focus_bands = spectra_of(focusing, forward)
        images = lax.map(lambda freq_index: image_one(freq_index, reflection, focus_bands), indices)
        upgoing = windowed(traces_of(images, inverse), onsets)
        upgoing_bands = spectra_of(upgoing, forward)
        returns = lax.map(lambda freq_index: return_one(freq_index, reflection, upgoing_bands), indices)
        focusing = focus_init + windowed(traces_of(returns, inverse), onsets)
    return (focusing, upgoing)
```

```python
import math

import jax
import jax.numpy as jnp
import ml_dtypes
import numpy as np
from jax import lax
from jax.experimental import pallas as pl
from jax.experimental.pallas import tpu as pltpu
from jax.sharding import PartitionSpec as P

NT = 512
ITERS = 2
LIMIT = 40 * 1024 * 1024


def split_table(table):
    high = table.astype(ml_dtypes.bfloat16)
    low = (table - high.astype(np.float32)).astype(ml_dtypes.bfloat16)
    return high, low


def band_tables(freq_count, time_count):
    harmonic = np.arange(1, freq_count + 1)
    phases = harmonic[:, None] * np.arange(time_count)[None, :] % time_count
    angles = phases * (2.0 * math.pi / time_count)
    factor = 1.0 / math.sqrt(time_count)
    cosines = np.stack([np.cos(angles), -np.sin(angles)], axis=1).reshape(2 * freq_count, time_count)
    forward = (cosines * factor).astype(np.float32)
    inverse = (cosines.T * (2.0 * factor)).astype(np.float32)
    return split_table(forward), split_table(inverse)


def dot(a, b):
    return jnp.dot(a, b, preferred_element_type=jnp.float32)


def dot_nt(a, b):
    return lax.dot_general(a, b, (((1,), (1,)), ((), ())), preferred_element_type=jnp.float32)


def halves(x):
    high = x.astype(jnp.bfloat16)
    return high, (x - high.astype(jnp.float32)).astype(jnp.bfloat16)


def table_times(high_ref, low_ref, x):
    if x.dtype == jnp.bfloat16:
        return dot(high_ref[...], x) + dot(low_ref[...], x)
    high, low = halves(x)
    return dot(high_ref[...], high) + dot(low_ref[...], high) + dot(high_ref[...], low)


def pick(rows_ref, row, step, count):
    return jnp.concatenate(
        [rows_ref[h, pl.ds(row, count, stride=step), :] for h in range(rows_ref.shape[0])], axis=1
    )


def place(rows_ref, row, step, value):
    for h in range(rows_ref.shape[0]):
        rows_ref[h, pl.ds(row, value.shape[0], stride=step), :] = value[:, h * 128 : (h + 1) * 128]


def fill(rows_ref, blocks):
    flat = blocks.reshape(rows_ref.shape[1], -1).astype(jnp.float32)
    for h in range(rows_ref.shape[0]):
        rows_ref[h] = flat[:, h * 128 : (h + 1) * 128]


def emptied(rows_ref, out_ref):
    flat = jnp.concatenate([rows_ref[h].astype(jnp.bfloat16) for h in range(rows_ref.shape[0])], axis=1)
    out_ref[...] = flat.reshape(out_ref.shape)


def image_kernel(step, bands_ref, refl_ref, out_ref, rows, bands):
    count = rows.shape[1] // step
    freqs = step // 2

    @pl.when(pl.program_id(0) == 0)
    def _():
        fill(rows, bands_ref[...])
        for j in range(freqs):
            for c in range(2):
                bands[j, c * count : (c + 1) * count, :] = pick(rows, 2 * j + c, step, count).astype(jnp.bfloat16)

    for j in range(freqs):
        a = dot_nt(bands[j], refl_ref[0, j])
        b = dot_nt(bands[j], refl_ref[1, j])
        place(rows, 2 * j, step, a[:count] - b[count:])
        place(rows, 2 * j + 1, step, b[:count] + a[count:])
    emptied(rows, out_ref)


def image_blocks(bands, reflection, panels):
    groups, height, width = bands.shape
    _, freqs, receivers, sources = reflection.shape
    block = receivers // panels
    step = 2 * freqs
    return pl.pallas_call(
        lambda *refs: image_kernel(step, *refs),
        grid=(panels,),
        in_specs=[
            pl.BlockSpec((groups, height, width), lambda p: (0, 0, 0)),
            pl.BlockSpec((2, freqs, block, sources), lambda p: (0, 0, p, 0)),
        ],
        out_specs=pl.BlockSpec((groups, 1, height, block), lambda p: (0, p, 0, 0)),
        out_shape=jax.ShapeDtypeStruct((groups, panels, height, block), jnp.bfloat16),
        scratch_shapes=[
            pltpu.VMEM((width // 128, groups * height, 128), jnp.float32),
            pltpu.VMEM((freqs, 2 * groups * height // step, width), jnp.bfloat16),
        ],
        compiler_params=pltpu.CompilerParams(vmem_limit_bytes=LIMIT),
        name="image_blocks",
    )(bands, reflection)


def return_kernel(step, bands_ref, refl_ref, out_ref, rows, total):
    count = rows.shape[1] // step
    freqs = step // 2
    panel = pl.program_id(0)

    @pl.when(panel == 0)
    def _():
        total[...] = jnp.zeros_like(total)

    fill(rows, bands_ref[...])
    for j in range(freqs):
        both = jnp.concatenate([pick(rows, 2 * j, step, count), pick(rows, 2 * j + 1, step, count)], axis=0)
        both = both.astype(jnp.bfloat16)
        a = dot(both, refl_ref[0, j])
        b = dot(both, refl_ref[1, j])
        total[j, 0] += a[:count] + b[count:]
        total[j, 1] += a[count:] - b[:count]

    @pl.when(panel == pl.num_programs(0) - 1)
    def _():
        for j in range(freqs):
            for c in range(2):
                place(rows, 2 * j + c, step, total[j, c])
        emptied(rows, out_ref)


def return_blocks(bands, reflection):
    groups, panels, height, width = bands.shape
    _, freqs, _, sources = reflection.shape
    step = 2 * freqs
    return pl.pallas_call(
        lambda *refs: return_kernel(step, *refs),
        grid=(panels,),
        in_specs=[
            pl.BlockSpec((groups, 1, height, width), lambda p: (0, p, 0, 0)),
            pl.BlockSpec((2, freqs, width, sources), lambda p: (0, 0, p, 0)),
        ],
        out_specs=pl.BlockSpec((groups, height, sources), lambda p: (0, 0, 0)),
        out_shape=jax.ShapeDtypeStruct((groups, height, sources), jnp.bfloat16),
        scratch_shapes=[
            pltpu.VMEM((width // 128, groups * height, 128), jnp.float32),
            pltpu.VMEM((freqs, 2, groups * height // step, sources), jnp.float32),
        ],
        compiler_params=pltpu.CompilerParams(vmem_limit_bytes=LIMIT),
        name="return_blocks",
    )(bands, reflection)


def windowed(traces, onsets_ref):
    samples = lax.broadcasted_iota(jnp.int32, traces.shape, 0)
    onsets = onsets_ref[0]
    return jnp.where((samples < onsets) | (samples > NT - onsets), traces, 0.0)


def table_specs(tables):
    return [pl.BlockSpec(t.shape, lambda v: (0, 0)) for pair in tables for t in pair]


def flat_tables(tables):
    return [jnp.asarray(t) for pair in tables for t in pair]


def start_kernel(high, low, traces_ref, first_ref, out_ref):
    spectra = table_times(high, low, traces_ref[...].reshape(NT, -1))
    first_ref[0] = spectra
    out_ref[...] = spectra.astype(jnp.bfloat16).reshape(out_ref.shape)


def start_bands(traces, forward, rows):
    blocks, count, share, width = traces.shape
    height = blocks * rows
    return pl.pallas_call(
        start_kernel,
        grid=(count,),
        in_specs=table_specs([forward])
        + [pl.BlockSpec((blocks, 1, share, width), lambda v: (0, v, 0, 0))],
        out_specs=[
            pl.BlockSpec((1, height, width), lambda v: (v, 0, 0)),
            pl.BlockSpec((blocks, rows, width), lambda v: (0, v, 0)),
        ],
        out_shape=[
            jax.ShapeDtypeStruct((count, height, width), jnp.float32),
            jax.ShapeDtypeStruct((blocks, count * rows, width), jnp.bfloat16),
        ],
        compiler_params=pltpu.CompilerParams(vmem_limit_bytes=LIMIT),
        name="start_bands",
    )(*flat_tables([forward]), traces)


def upgoing_kernel(with_traces, ih, il, fh, fl, onsets_ref, parts_ref, *outs):
    groups, panels, rows, width = parts_ref.shape
    images = parts_ref[:, 0].astype(jnp.float32)
    for p in range(1, panels):
        images = images + parts_ref[:, p].astype(jnp.float32)
    traces = windowed(table_times(ih, il, images.reshape(groups * rows, width)), onsets_ref)
    spectra = table_times(fh, fl, traces).astype(jnp.bfloat16).reshape(groups, rows, width)
    for p in range(panels):
        outs[0][:, p] = spectra
    if with_traces:
        outs[1][...] = traces.astype(jnp.bfloat16).reshape(outs[1].shape)


def upgoing_blocks(parts, onsets, tables, rows, with_traces):
    groups, panels, height, width = parts.shape
    count = height // rows
    share = NT // groups
    block = pl.BlockSpec((groups, panels, rows, width), lambda v: (0, 0, v, 0))
    out_specs = [block]
    out_shape = [jax.ShapeDtypeStruct(parts.shape, jnp.bfloat16)]
    if with_traces:
        out_specs.append(pl.BlockSpec((groups, 1, share, width), lambda v: (0, v, 0, 0)))
        out_shape.append(jax.ShapeDtypeStruct((groups, count, share, width), jnp.bfloat16))
    return pl.pallas_call(
        lambda *refs: upgoing_kernel(with_traces, *refs),
        grid=(count,),
        in_specs=table_specs(tables) + [pl.BlockSpec((1, 1, width), lambda v: (v, 0, 0)), block],
        out_specs=out_specs,
        out_shape=out_shape,
        compiler_params=pltpu.CompilerParams(vmem_limit_bytes=LIMIT),
        name="upgoing_blocks",
    )(*flat_tables(tables), onsets, parts)


def focus_kernel(ih, il, fh, fl, onsets_ref, first_ref, returns_ref, out_ref):
    groups, rows, width = returns_ref.shape
    traces = windowed(table_times(ih, il, returns_ref[...].reshape(groups * rows, width)), onsets_ref)
    spectra = first_ref[0] + table_times(fh, fl, traces)
    out_ref[...] = spectra.astype(jnp.bfloat16).reshape(out_ref.shape)


def focus_blocks(returns, first, onsets, tables, rows):
    groups, height, width = returns.shape
    block = pl.BlockSpec((groups, rows, width), lambda v: (0, v, 0))
    return pl.pallas_call(
        focus_kernel,
        grid=(height // rows,),
        in_specs=table_specs(tables)
        + [
            pl.BlockSpec((1, 1, width), lambda v: (v, 0, 0)),
            pl.BlockSpec((1, groups * rows, width), lambda v: (v, 0, 0)),
            block,
        ],
        out_specs=block,
        out_shape=jax.ShapeDtypeStruct(returns.shape, jnp.bfloat16),
        compiler_params=pltpu.CompilerParams(vmem_limit_bytes=LIMIT),
        name="focus_blocks",
    )(*flat_tables(tables), onsets, first, returns)


def trace_kernel(ih, il, onsets_ref, returns_ref, out_ref):
    groups, rows, width = returns_ref.shape
    traces = windowed(table_times(ih, il, returns_ref[...].reshape(groups * rows, width)), onsets_ref)
    out_ref[...] = traces.astype(jnp.bfloat16).reshape(out_ref.shape)


def trace_blocks(returns, onsets, inverse, rows):
    groups, height, width = returns.shape
    count = height // rows
    share = NT // groups
    return pl.pallas_call(
        trace_kernel,
        grid=(count,),
        in_specs=table_specs([inverse])
        + [
            pl.BlockSpec((1, 1, width), lambda v: (v, 0, 0)),
            pl.BlockSpec((groups, rows, width), lambda v: (0, v, 0)),
        ],
        out_specs=pl.BlockSpec((groups, 1, share, width), lambda v: (0, v, 0, 0)),
        out_shape=jax.ShapeDtypeStruct((groups, count, share, width), jnp.bfloat16),
        compiler_params=pltpu.CompilerParams(vmem_limit_bytes=LIMIT),
        name="trace_blocks",
    )(*flat_tables([inverse]), onsets, returns)


def exchange(blocks, axis):
    return lax.all_to_all(blocks, axis, split_axis=0, concat_axis=0, tiled=True)


def local(reflection, focus_init, onsets):
    groups = lax.axis_size("freq")
    panels = lax.axis_size("panel")
    _, freqs, _, _ = reflection.shape
    share, sources, width = focus_init.shape
    count = sources // groups
    rows = 2 * freqs
    forward, inverse = band_tables(freqs * groups, NT)
    tables = [inverse, forward]
    own_onsets = lax.dynamic_slice_in_dim(onsets, lax.axis_index("freq") * count, count, 0)
    own_onsets = own_onsets.reshape(count, 1, width)

    def to_all(blocks):
        flat = blocks.reshape((groups * panels,) + blocks.shape[2:])
        return exchange(flat, ("freq", "panel")).reshape(blocks.shape)

    def to_time(blocks):
        samples = exchange(blocks, "freq")
        return jnp.transpose(samples, (2, 0, 1, 3)).reshape(share, sources, width).astype(jnp.float32)

    sent = focus_init.astype(jnp.bfloat16).reshape(share, groups, count, width).transpose(1, 2, 0, 3)
    first, blocks = start_bands(exchange(sent, "freq"), forward, rows)
    for iteration in range(ITERS):
        last = iteration == ITERS - 1
        bands = exchange(blocks, "freq")
        parts = to_all(image_blocks(bands, reflection, panels))
        outs = upgoing_blocks(parts, own_onsets, tables, rows, last)
        returns = exchange(return_blocks(to_all(outs[0]), reflection), "freq")
        if last:
            upgoing = to_time(outs[1])
            focusing = focus_init + to_time(trace_blocks(returns, own_onsets, inverse, rows))
        else:
            blocks = focus_blocks(returns, first, own_onsets, tables, rows)
    return (focusing, upgoing)


def solution(mesh):
    placed = (P(None, "freq", None, "panel"), P("freq", None, "panel"), P(None, "panel"))
    return jax.shard_map(
        local,
        mesh=mesh,
        in_specs=placed,
        out_specs=(P("freq", None, "panel"), P("freq", None, "panel")),
        check_vma=False,
    )
```

```python
import math

import jax
import jax.numpy as jnp
import ml_dtypes
import numpy as np
from jax import lax
from jax.experimental import pallas as pl
from jax.experimental.pallas import tpu as pltpu
from jax.sharding import PartitionSpec as P

NT = 512
ITERS = 2
MIB = 1024 * 1024


def split_table(table):
    high = table.astype(ml_dtypes.bfloat16)
    low = (table - high.astype(np.float32)).astype(ml_dtypes.bfloat16)
    return high, low


def band_tables(freq_count, time_count):
    harmonic = np.arange(1, freq_count + 1)
    phases = harmonic[:, None] * np.arange(time_count)[None, :] % time_count
    angles = phases * (2.0 * math.pi / time_count)
    factor = 1.0 / math.sqrt(time_count)
    cosines = np.stack([np.cos(angles), -np.sin(angles)], axis=1).reshape(2 * freq_count, time_count)
    forward = (cosines * factor).astype(np.float32)
    inverse = (cosines.T * (2.0 * factor)).astype(np.float32)
    return split_table(forward), split_table(inverse)


def dot(a, b):
    return jnp.dot(a, b, preferred_element_type=jnp.float32)


def dot_nt(a, b):
    return lax.dot_general(a, b, (((1,), (1,)), ((), ())), preferred_element_type=jnp.float32)


def halves(x):
    high = x.astype(jnp.bfloat16)
    return high, (x - high.astype(jnp.float32)).astype(jnp.bfloat16)


def table_times(high_ref, low_ref, x):
    if x.dtype == jnp.bfloat16:
        return dot(high_ref[...], x) + dot(low_ref[...], x)
    high, low = halves(x)
    return dot(high_ref[...], high) + dot(low_ref[...], high) + dot(high_ref[...], low)


def pick(rows_ref, row, step, count):
    return jnp.concatenate(
        [rows_ref[h, pl.ds(row, count, stride=step), :] for h in range(rows_ref.shape[0])], axis=1
    )


def place(rows_ref, row, step, value):
    for h in range(rows_ref.shape[0]):
        rows_ref[h, pl.ds(row, value.shape[0], stride=step), :] = value[:, h * 128 : (h + 1) * 128]


def fill(rows_ref, blocks):
    flat = blocks.reshape(rows_ref.shape[1], -1).astype(jnp.float32)
    for h in range(rows_ref.shape[0]):
        rows_ref[h] = flat[:, h * 128 : (h + 1) * 128]


def emptied(rows_ref, out_ref):
    flat = jnp.concatenate([rows_ref[h].astype(jnp.bfloat16) for h in range(rows_ref.shape[0])], axis=1)
    out_ref[...] = flat.reshape(out_ref.shape)


def image_kernel(first, bands_ref, refl_ref, out_ref, *more):
    held_ref = more[0] if first else refl_ref
    rows, direct, crossed = more[first : first + 3]
    _, freqs, height, width = refl_ref.shape
    step = 2 * freqs
    count = rows.shape[1] // step
    groups, panels, block, share = out_ref.shape

    copies = []
    if first:
        for p in range(panels):
            part = (slice(None), slice(None), pl.ds(p * share, share))
            copies.append(pltpu.make_async_copy(refl_ref.at[part], held_ref.at[part], more[-1].at[p]))
            copies[-1].start()

    fill(rows, bands_ref[...])
    for j in range(freqs):
        real, imag = pick(rows, 2 * j, step, count), pick(rows, 2 * j + 1, step, count)
        direct[j] = jnp.concatenate([real, imag], axis=0).astype(jnp.bfloat16)
        crossed[j] = jnp.concatenate([-imag, real], axis=0).astype(jnp.bfloat16)

    for p in range(panels):
        if first:
            copies[p].wait()
        at = slice(p * share, (p + 1) * share)
        images = [
            dot_nt(direct[j], held_ref[0, j, at]) + dot_nt(crossed[j], held_ref[1, j, at]) for j in range(freqs)
        ]
        images = jnp.stack(images).reshape(step, count, share)
        out_ref[:, p] = jnp.swapaxes(images, 0, 1).astype(jnp.bfloat16).reshape(groups, block, share)


IN_VMEM = pl.BlockSpec(memory_space=pltpu.VMEM)


def call(kernel, name, out_shape, args, scratch=(), specs=None, flops=0):
    size = sum(a.size * a.dtype.itemsize for a in args)
    return pl.pallas_call(
        kernel,
        in_specs=specs or [IN_VMEM] * len(args),
        out_specs=jax.tree.map(lambda _: IN_VMEM, out_shape),
        out_shape=out_shape,
        scratch_shapes=list(scratch),
        compiler_params=pltpu.CompilerParams(vmem_limit_bytes=16 * MIB),
        cost_estimate=pl.CostEstimate(flops=flops, bytes_accessed=2 * size, transcendentals=0),
        name=name,
    )(*args)


def image_blocks(bands, reflection, panels, first):
    groups, height, width = bands.shape
    _, freqs, receivers, _ = reflection.shape
    count = groups * height // (2 * freqs)
    out_shape = [jax.ShapeDtypeStruct((groups, panels, height, receivers // panels), jnp.bfloat16)]
    scratch = [
        pltpu.VMEM((width // 128, groups * height, 128), jnp.float32),
        pltpu.VMEM((freqs, 2 * count, width), jnp.bfloat16),
        pltpu.VMEM((freqs, 2 * count, width), jnp.bfloat16),
    ]
    specs = None
    if first:
        out_shape.append(pltpu.VMEM(reflection.shape, reflection.dtype))
        scratch.append(pltpu.SemaphoreType.DMA((panels,)))
        specs = [IN_VMEM, pl.BlockSpec(memory_space=pltpu.HBM)]
        reflection = pltpu.with_memory_space_constraint(reflection, pltpu.HBM)
    return call(
        lambda *refs: image_kernel(int(first), *refs),
        "image_blocks",
        out_shape,
        (bands, reflection),
        scratch,
        specs,
        flops=4 * reflection.size * count,
    )


def return_kernel(bands_ref, refl_ref, *more):
    out_ref, rows, results = more[-3:]
    groups, panels, block, width = bands_ref.shape
    freqs = refl_ref.shape[1]
    step = 2 * freqs
    count = groups * block // step
    lanes = width // 128

    for p in range(panels):
        flat = bands_ref[:, p].reshape(groups * block, width).astype(jnp.float32)
        for h in range(lanes):
            rows[p * lanes + h] = flat[:, h * 128 : (h + 1) * 128]

    for j in range(freqs):
        total = None
        for p in range(panels):
            of_panel = rows.at[pl.ds(p * lanes, lanes)]
            real = pick(of_panel, 2 * j, step, count)
            imag = pick(of_panel, 2 * j + 1, step, count)
            direct = jnp.concatenate([real, imag], axis=0).astype(jnp.bfloat16)
            crossed = jnp.concatenate([imag, -real], axis=0).astype(jnp.bfloat16)
            at = slice(p * width, (p + 1) * width)
            part = dot(direct, refl_ref[0, j, at]) + dot(crossed, refl_ref[1, j, at])
            total = part if total is None else total + part
        place(results, 2 * j, step, total[:count])
        place(results, 2 * j + 1, step, total[count:])
    emptied(results, out_ref.at[:, :block])
    if len(more) > 3:
        out_ref[:, block:] = more[0][...].reshape(groups, -1, width)


def return_blocks(bands, reflection, traces=()):
    groups, panels, height, width = bands.shape
    _, freqs, _, sources = reflection.shape
    more = sum(t.size // (groups * width) for t in traces)
    return call(
        return_kernel,
        "return_blocks",
        jax.ShapeDtypeStruct((groups, height + more, sources), jnp.bfloat16),
        (bands, reflection, *traces),
        [
            pltpu.VMEM((panels * width // 128, groups * height, 128), jnp.float32),
            pltpu.VMEM((sources // 128, groups * height, 128), jnp.float32),
        ],
        flops=4 * reflection.size * groups * height // (2 * freqs),
    )


def windowed(traces, onsets_ref, v):
    count = onsets_ref.shape[0] // lax.axis_size("freq")
    onsets = onsets_ref[pl.ds(lax.axis_index("freq") * count + v, 1), :]
    samples = lax.broadcasted_iota(jnp.int32, traces.shape, 0)
    return jnp.where((samples < onsets) | (samples > NT - onsets), traces, 0.0)


def start_kernel(high, low, traces_ref, first_ref, out_ref):
    blocks, count, share, width = traces_ref.shape
    rows = out_ref.shape[1] // count
    for v in range(count):
        spectra = table_times(high, low, traces_ref[:, v].reshape(blocks * share, width))
        first_ref[v] = spectra
        out_ref[:, v * rows : (v + 1) * rows] = spectra.astype(jnp.bfloat16).reshape(blocks, rows, width)


def start_bands(traces, forward, rows):
    blocks, count, _, width = traces.shape
    return call(
        start_kernel,
        "start_bands",
        [
            pltpu.VMEM((count, blocks * rows, width), jnp.float32),
            jax.ShapeDtypeStruct((blocks, count * rows, width), jnp.bfloat16),
        ],
        (*forward, traces),
    )


def upgoing_kernel(rows, ih, il, fh, fl, onsets_ref, parts_ref, out_ref, *traces_ref):
    groups, panels, height, width = parts_ref.shape
    for v in range(height // rows):
        at = slice(v * rows, (v + 1) * rows)
        images = parts_ref[:, 0, at].astype(jnp.float32)
        for p in range(1, panels):
            images = images + parts_ref[:, p, at].astype(jnp.float32)
        traces = windowed(table_times(ih, il, images.reshape(groups * rows, width)), onsets_ref, v)
        spectra = table_times(fh, fl, traces).astype(jnp.bfloat16).reshape(groups, rows, width)
        for p in range(panels):
            out_ref[:, p, at] = spectra
        for ref in traces_ref:
            ref[:, v] = traces.astype(jnp.bfloat16).reshape(groups, -1, width)


def upgoing_blocks(parts, onsets, tables, rows, with_traces):
    groups, panels, height, width = parts.shape
    out_shape = [jax.ShapeDtypeStruct(parts.shape, jnp.bfloat16)]
    if with_traces:
        out_shape.append(jax.ShapeDtypeStruct((groups, height // rows, NT // groups, width), jnp.bfloat16))
    return call(
        lambda *refs: upgoing_kernel(rows, *refs), "upgoing_blocks", out_shape, (*tables, onsets, parts)
    )


def focus_kernel(rows, ih, il, fh, fl, onsets_ref, first_ref, returns_ref, out_ref):
    groups, height, width = returns_ref.shape
    for v in range(height // rows):
        at = slice(v * rows, (v + 1) * rows)
        returns = returns_ref[:, at].reshape(groups * rows, width)
        traces = windowed(table_times(ih, il, returns), onsets_ref, v)
        spectra = first_ref[v] + table_times(fh, fl, traces)
        out_ref[:, at] = spectra.astype(jnp.bfloat16).reshape(groups, rows, width)


def focus_blocks(returns, first, onsets, tables, rows):
    return call(
        lambda *refs: focus_kernel(rows, *refs),
        "focus_blocks",
        jax.ShapeDtypeStruct(returns.shape, jnp.bfloat16),
        (*tables, onsets, first, returns),
    )


def trace_kernel(rows, ih, il, onsets_ref, returns_ref, out_ref):
    groups, count, _, width = out_ref.shape
    for v in range(count):
        returns = returns_ref[:, v * rows : (v + 1) * rows].reshape(groups * rows, width)
        traces = windowed(table_times(ih, il, returns), onsets_ref, v)
        out_ref[:, v] = traces.astype(jnp.bfloat16).reshape(groups, -1, width)


def trace_blocks(returns, onsets, inverse, rows, count):
    groups, _, width = returns.shape
    return call(
        lambda *refs: trace_kernel(rows, *refs),
        "trace_blocks",
        jax.ShapeDtypeStruct((groups, count, NT // groups, width), jnp.bfloat16),
        (*inverse, onsets, returns),
    )


def exchange(blocks, axis):
    return lax.all_to_all(blocks, axis, split_axis=0, concat_axis=0, tiled=True)


def local(reflection, focus_init, onsets):
    groups = lax.axis_size("freq")
    panels = lax.axis_size("panel")
    freqs = reflection.shape[1]
    share, sources, width = focus_init.shape
    count = sources // groups
    rows = 2 * freqs
    forward, inverse = [[jnp.asarray(t) for t in pair] for pair in band_tables(freqs * groups, NT)]
    tables = inverse + forward

    def to_all(blocks):
        flat = blocks.reshape((groups * panels,) + blocks.shape[2:])
        return exchange(flat, ("freq", "panel")).reshape(blocks.shape)

    def in_time(samples):
        samples = samples.reshape(groups, count, share, width)
        return jnp.transpose(samples, (2, 0, 1, 3)).reshape(share, sources, width).astype(jnp.float32)

    sent = focus_init.astype(jnp.bfloat16).reshape(share, groups, count, width).transpose(1, 2, 0, 3)
    first, blocks = start_bands(exchange(sent, "freq"), forward, rows)
    for iteration in range(ITERS):
        last = iteration == ITERS - 1
        bands = exchange(blocks, "freq")
        images = image_blocks(bands, reflection, panels, iteration == 0)
        if iteration == 0:
            reflection = images[1]
        spectra, *traces = upgoing_blocks(to_all(images[0]), onsets, tables, rows, last)
        returns = exchange(return_blocks(to_all(spectra), reflection, traces), "freq")
        if last:
            upgoing = in_time(returns[:, count * rows :])
            traces = trace_blocks(returns, onsets, inverse, rows, count)
            focusing = focus_init + in_time(exchange(traces, "freq"))
        else:
            blocks = focus_blocks(returns, first, onsets, tables, rows)
    return (focusing, upgoing)


def solution(mesh):
    placed = (P(None, "freq", None, "panel"), P("freq", None, "panel"), P(None, "panel"))
    return jax.shard_map(
        local,
        mesh=mesh,
        in_specs=placed,
        out_specs=(P("freq", None, "panel"), P("freq", None, "panel")),
        check_vma=False,
    )
```

```python
import math

import jax
import jax.numpy as jnp
import ml_dtypes
import numpy as np
from jax import lax
from jax.experimental import pallas as pl
from jax.experimental.pallas import tpu as pltpu
from jax.sharding import PartitionSpec as P

NT = 512
ITERS = 2
MIB = 1024 * 1024


def split_table(table):
    high = table.astype(ml_dtypes.bfloat16)
    low = (table - high.astype(np.float32)).astype(ml_dtypes.bfloat16)
    return high, low


def band_tables(freq_count, time_count):
    harmonic = np.arange(1, freq_count + 1)
    phases = harmonic[:, None] * np.arange(time_count)[None, :] % time_count
    angles = phases * (2.0 * math.pi / time_count)
    factor = 1.0 / math.sqrt(time_count)
    cosines = np.stack([np.cos(angles), -np.sin(angles)], axis=1).reshape(2 * freq_count, time_count)
    forward = (cosines * factor).astype(np.float32)
    inverse = (cosines.T * (2.0 * factor)).astype(np.float32)
    return split_table(forward), split_table(inverse)


def dot(a, b):
    return jnp.dot(a, b, preferred_element_type=jnp.float32)


def dot_nt(a, b):
    return lax.dot_general(a, b, (((1,), (1,)), ((), ())), preferred_element_type=jnp.float32)


def halves(x):
    high = x.astype(jnp.bfloat16)
    return high, (x - high.astype(jnp.float32)).astype(jnp.bfloat16)


def table_times(high_ref, low_ref, x):
    if x.dtype == jnp.bfloat16:
        return dot(high_ref[...], x) + dot(low_ref[...], x)
    high, low = halves(x)
    return dot(high_ref[...], high) + dot(low_ref[...], high) + dot(high_ref[...], low)


def pick(rows_ref, row, step, count):
    return jnp.concatenate(
        [rows_ref[h, pl.ds(row, count, stride=step), :] for h in range(rows_ref.shape[0])], axis=1
    )


def place(rows_ref, row, step, value):
    for h in range(rows_ref.shape[0]):
        rows_ref[h, pl.ds(row, value.shape[0], stride=step), :] = value[:, h * 128 : (h + 1) * 128]


def fill(rows_ref, blocks):
    flat = blocks.reshape(rows_ref.shape[1], -1).astype(jnp.float32)
    for h in range(rows_ref.shape[0]):
        rows_ref[h] = flat[:, h * 128 : (h + 1) * 128]


def emptied(rows_ref, out_ref):
    flat = jnp.concatenate([rows_ref[h].astype(jnp.bfloat16) for h in range(rows_ref.shape[0])], axis=1)
    out_ref[...] = flat.reshape(out_ref.shape)


EARLY = (5, 7, 6)
LATE = (1, 3, 4, 2, 0)


def fetch(order, refl_ref, held_ref, sems):
    share = held_ref.shape[2] // len(order)
    copies = []
    for i, k in enumerate(order):
        start = pl.multiple_of((lax.axis_index("panel") ^ k) * share, share)
        copies.append(
            pltpu.make_async_copy(
                refl_ref.at[:, :, pl.ds(start, share)], held_ref.at[:, :, pl.ds(i * share, share)], sems.at[i]
            )
        )
        copies[-1].start()
    return copies


def image_kernel(order, spread, first, bands_ref, *refs):
    if spread:
        refl_ref, *refs = refs
    else:
        crossed, refl_ref, *refs = refs
        direct = bands_ref
    out_refs, refs = refs[: len(order)], refs[len(order) :]
    if spread:
        direct, crossed, *refs = refs
    held_ref, copies = refl_ref, []
    if first:
        held_ref, *refs = refs
        copies = fetch(order, refl_ref, held_ref, refs[-1])

    _, freqs, height, _ = held_ref.shape
    step = 2 * freqs
    groups, block, share = out_refs[0].shape
    count = groups * block // step
    if spread:
        rows = refs[0]
        fill(rows, bands_ref[...])
        for j in range(freqs):
            real, imag = pick(rows, 2 * j, step, count), pick(rows, 2 * j + 1, step, count)
            direct[j] = jnp.concatenate([real, imag], axis=0).astype(jnp.bfloat16)
            crossed[j] = jnp.concatenate([-imag, real], axis=0).astype(jnp.bfloat16)

    for i, out_ref in enumerate(out_refs):
        if first:
            copies[i].wait()
        at = slice(i * share, (i + 1) * share)
        images = [
            dot_nt(direct[j], held_ref[0, j, at]) + dot_nt(crossed[j], held_ref[1, j, at]) for j in range(freqs)
        ]
        images = jnp.stack(images).reshape(step, count, share)
        out_ref[...] = jnp.swapaxes(images, 0, 1).astype(jnp.bfloat16).reshape(groups, block, share)


IN_VMEM = pl.BlockSpec(memory_space=pltpu.VMEM)


def call(kernel, name, out_shape, args, scratch=(), specs=None, flops=0):
    size = sum(a.size * a.dtype.itemsize for a in args)
    return pl.pallas_call(
        kernel,
        in_specs=specs or [IN_VMEM] * len(args),
        out_specs=jax.tree.map(lambda _: IN_VMEM, out_shape),
        out_shape=out_shape,
        scratch_shapes=list(scratch),
        compiler_params=pltpu.CompilerParams(vmem_limit_bytes=16 * MIB),
        cost_estimate=pl.CostEstimate(flops=flops, bytes_accessed=2 * size, transcendentals=0),
        name=name,
    )(*args)


def image_blocks(order, sources, reflection, panels, first):
    spread = len(sources) == 1
    _, freqs, receivers, width = reflection.shape
    share = receivers // (panels if first else len(order))
    if spread:
        groups, height, _ = sources[0].shape
        count = groups * height // (2 * freqs)
        by_freq = jax.ShapeDtypeStruct((freqs, 2 * count, width), jnp.bfloat16)
    else:
        count = sources[0].shape[1] // 2
        height = 2 * freqs * count // lax.axis_size("freq")
        groups = lax.axis_size("freq")
    out_shape = [jax.ShapeDtypeStruct((groups, height, share), jnp.bfloat16)] * len(order)
    scratch = []
    if spread:
        out_shape += [by_freq, by_freq]
        scratch.append(pltpu.VMEM((width // 128, groups * height, 128), jnp.float32))
    specs = None
    if first:
        out_shape.append(pltpu.VMEM((2, freqs, share * len(order), width), reflection.dtype))
        scratch.append(pltpu.SemaphoreType.DMA((len(order),)))
        specs = [IN_VMEM] * len(sources) + [pl.BlockSpec(memory_space=pltpu.HBM)]
        reflection = pltpu.with_memory_space_constraint(reflection, pltpu.HBM)
    outs = call(
        lambda *refs: image_kernel(order, spread, first, *refs),
        "image_blocks",
        out_shape,
        (*sources, reflection),
        scratch,
        specs,
        flops=4 * 2 * freqs * share * len(order) * width * count,
    )
    blocks, outs = outs[: len(order)], outs[len(order) :]
    return blocks, outs[:2] if spread else sources, outs[-1] if first else reflection


def return_kernel(panels, final, *refs):
    blocks, refl_ref, refs = refs[:panels], refs[panels], refs[panels + 1 :]
    groups, block, width = blocks[0].shape
    freqs = refl_ref.shape[1]
    step = 2 * freqs
    count = groups * block // step
    lanes = width // 128
    if final:
        before, *more, out_ref, rows, results = refs
    else:
        total_ref, rows = refs

    for p in range(panels):
        flat = blocks[p][...].reshape(groups * block, width).astype(jnp.float32)
        for h in range(lanes):
            rows[p * lanes + h] = flat[:, h * 128 : (h + 1) * 128]

    for j in range(freqs):
        total = before[j] if final else None
        for p in range(panels):
            of_panel = rows.at[pl.ds(p * lanes, lanes)]
            real = pick(of_panel, 2 * j, step, count)
            imag = pick(of_panel, 2 * j + 1, step, count)
            direct = jnp.concatenate([real, imag], axis=0).astype(jnp.bfloat16)
            crossed = jnp.concatenate([imag, -real], axis=0).astype(jnp.bfloat16)
            at = slice(p * width, (p + 1) * width)
            part = dot(direct, refl_ref[0, j, at]) + dot(crossed, refl_ref[1, j, at])
            total = part if total is None else total + part
        if final:
            place(results, 2 * j, step, total[:count])
            place(results, 2 * j + 1, step, total[count:])
        else:
            total_ref[j] = total
    if final:
        emptied(results, out_ref.at[:, :block])
        for ref in more:
            out_ref[:, block:] = ref[...].reshape(groups, -1, width)


def return_blocks(blocks, reflection, before=None, traces=()):
    panels = len(blocks)
    groups, height, width = blocks[0].shape
    _, freqs, _, sources = reflection.shape
    count = groups * height // (2 * freqs)
    final = before is not None
    more = sum(t.size // (groups * width) for t in traces)
    scratch = [pltpu.VMEM((panels * width // 128, groups * height, 128), jnp.float32)]
    if final:
        out_shape = jax.ShapeDtypeStruct((groups, height + more, sources), jnp.bfloat16)
        scratch.append(pltpu.VMEM((sources // 128, groups * height, 128), jnp.float32))
    else:
        out_shape = jax.ShapeDtypeStruct((freqs, 2 * count, sources), jnp.float32)
    return call(
        lambda *refs: return_kernel(panels, final, *refs),
        "return_blocks",
        out_shape,
        (*blocks, reflection, *([before] if final else []), *traces),
        scratch,
        flops=4 * reflection.size * count,
    )


def windowed(traces, onsets_ref, v):
    count = onsets_ref.shape[0] // lax.axis_size("freq")
    onsets = onsets_ref[pl.ds(lax.axis_index("freq") * count + v, 1), :]
    samples = lax.broadcasted_iota(jnp.int32, traces.shape, 0)
    return jnp.where((samples < onsets) | (samples > NT - onsets), traces, 0.0)


def start_kernel(high, low, traces_ref, first_ref, out_ref):
    blocks, count, share, width = traces_ref.shape
    rows = out_ref.shape[1] // count
    for v in range(count):
        spectra = table_times(high, low, traces_ref[:, v].reshape(blocks * share, width))
        first_ref[v] = spectra
        out_ref[:, v * rows : (v + 1) * rows] = spectra.astype(jnp.bfloat16).reshape(blocks, rows, width)


def start_bands(traces, forward, rows):
    blocks, count, _, width = traces.shape
    return call(
        start_kernel,
        "start_bands",
        [
            pltpu.VMEM((count, blocks * rows, width), jnp.float32),
            jax.ShapeDtypeStruct((blocks, count * rows, width), jnp.bfloat16),
        ],
        (*forward, traces),
    )


def upgoing_kernel(rows, ih, il, fh, fl, onsets_ref, images_ref, out_ref, *traces_ref):
    groups, height, width = images_ref.shape
    for v in range(height // rows):
        at = slice(v * rows, (v + 1) * rows)
        images = images_ref[:, at].reshape(groups * rows, width)
        traces = windowed(table_times(ih, il, images), onsets_ref, v)
        out_ref[:, at] = table_times(fh, fl, traces).astype(jnp.bfloat16).reshape(groups, rows, width)
        for ref in traces_ref:
            ref[:, v] = traces.astype(jnp.bfloat16).reshape(groups, -1, width)


def upgoing_blocks(images, onsets, tables, rows, with_traces):
    groups, height, width = images.shape
    out_shape = [jax.ShapeDtypeStruct(images.shape, jnp.bfloat16)]
    if with_traces:
        out_shape.append(jax.ShapeDtypeStruct((groups, height // rows, NT // groups, width), jnp.bfloat16))
    return call(
        lambda *refs: upgoing_kernel(rows, *refs), "upgoing_blocks", out_shape, (*tables, onsets, images)
    )


def focus_kernel(rows, ih, il, fh, fl, onsets_ref, first_ref, returns_ref, out_ref):
    groups, height, width = returns_ref.shape
    for v in range(height // rows):
        at = slice(v * rows, (v + 1) * rows)
        returns = returns_ref[:, at].reshape(groups * rows, width)
        traces = windowed(table_times(ih, il, returns), onsets_ref, v)
        spectra = first_ref[v] + table_times(fh, fl, traces)
        out_ref[:, at] = spectra.astype(jnp.bfloat16).reshape(groups, rows, width)


def focus_blocks(returns, first, onsets, tables, rows):
    return call(
        lambda *refs: focus_kernel(rows, *refs),
        "focus_blocks",
        jax.ShapeDtypeStruct(returns.shape, jnp.bfloat16),
        (*tables, onsets, first, returns),
    )


def trace_kernel(rows, ih, il, onsets_ref, returns_ref, out_ref):
    groups, count, _, width = out_ref.shape
    for v in range(count):
        returns = returns_ref[:, v * rows : (v + 1) * rows].reshape(groups * rows, width)
        traces = windowed(table_times(ih, il, returns), onsets_ref, v)
        out_ref[:, v] = traces.astype(jnp.bfloat16).reshape(groups, -1, width)


def trace_blocks(returns, onsets, inverse, rows, count):
    groups, _, width = returns.shape
    return call(
        lambda *refs: trace_kernel(rows, *refs),
        "trace_blocks",
        jax.ShapeDtypeStruct((groups, count, NT // groups, width), jnp.bfloat16),
        (*inverse, onsets, returns),
    )


def exchange(blocks, axis):
    return lax.all_to_all(blocks, axis, split_axis=0, concat_axis=0, tiled=True)


def send(block, k):
    return lax.ppermute(block, "panel", [(i, i ^ k) for i in range(lax.axis_size("panel"))])


def added(*blocks):
    total = blocks[0].astype(jnp.float32)
    for block in blocks[1:]:
        total = total + block.astype(jnp.float32)
    return total.astype(jnp.bfloat16)


def local(reflection, focus_init, onsets):
    groups = lax.axis_size("freq")
    panels = lax.axis_size("panel")
    freqs = reflection.shape[1]
    share, sources, width = focus_init.shape
    count = sources // groups
    rows = 2 * freqs
    forward, inverse = [[jnp.asarray(t) for t in pair] for pair in band_tables(freqs * groups, NT)]
    tables = inverse + forward

    def in_time(samples):
        samples = samples.reshape(groups, count, share, width)
        return jnp.transpose(samples, (2, 0, 1, 3)).reshape(share, sources, width).astype(jnp.float32)

    sent = focus_init.astype(jnp.bfloat16).reshape(share, groups, count, width).transpose(1, 2, 0, 3)
    first, blocks = start_bands(exchange(sent, "freq"), forward, rows)
    early = late = reflection
    for iteration in range(ITERS):
        is_first, last = iteration == 0, iteration == ITERS - 1
        bands = exchange(blocks, "freq")
        (b5, b7, b6), by_freq, early = image_blocks(EARLY, (bands,), early, panels, is_first)
        r5, r7, r6 = send(b5, 1), send(b7, 3), send(b6, 4)
        (b1, b3, b4, b2, b0), _, late = image_blocks(LATE, tuple(by_freq), late, panels, is_first)
        s1, s3 = send(b1, 1), send(b3, 3)
        s2, s4 = send(added(b2, r6), 2), send(added(b4, r5, r7), 4)
        images = exchange(added(b0, s1, s3, s2, s4), "freq")
        spectra, *traces = upgoing_blocks(images, onsets, tables, rows, last)
        m0 = exchange(spectra, "freq")
        m2, m4, m1, m3 = send(m0, 2), send(m0, 4), send(m0, 1), send(m0, 3)
        m6, m5, m7 = send(m2, 4), send(m4, 1), send(m4, 3)
        partial = return_blocks((m1, m3, m4, m2, m0), late)
        returns = exchange(return_blocks((m5, m7, m6), early, partial, traces), "freq")
        if last:
            upgoing = in_time(returns[:, count * rows :])
            traces = trace_blocks(returns, onsets, inverse, rows, count)
            focusing = focus_init + in_time(exchange(traces, "freq"))
        else:
            blocks = focus_blocks(returns, first, onsets, tables, rows)
    return (focusing, upgoing)


def solution(mesh):
    placed = (P(None, "freq", None, "panel"), P("freq", None, "panel"), P(None, "panel"))
    return jax.shard_map(
        local,
        mesh=mesh,
        in_specs=placed,
        out_specs=(P("freq", None, "panel"), P("freq", None, "panel")),
        check_vma=False,
    )
```

```python
import math

import jax
import jax.numpy as jnp
import ml_dtypes
import numpy as np
from jax import lax
from jax.experimental import pallas as pl
from jax.experimental.pallas import tpu as pltpu
from jax.sharding import PartitionSpec as P

NT = 512
ITERS = 2
MIB = 1024 * 1024


def split_table(table):
    high = table.astype(ml_dtypes.bfloat16)
    low = (table - high.astype(np.float32)).astype(ml_dtypes.bfloat16)
    return high, low


def band_tables(freq_count, time_count):
    harmonic = np.arange(1, freq_count + 1)
    phases = harmonic[:, None] * np.arange(time_count)[None, :] % time_count
    angles = phases * (2.0 * math.pi / time_count)
    factor = 1.0 / math.sqrt(time_count)
    cosines = np.stack([np.cos(angles), -np.sin(angles)], axis=1).reshape(2 * freq_count, time_count)
    forward = (cosines * factor).astype(np.float32)
    inverse = (cosines.T * (2.0 * factor)).astype(np.float32)
    return split_table(forward), split_table(inverse)


def dot(a, b):
    return jnp.dot(a, b, preferred_element_type=jnp.float32)


def dot_nt(a, b):
    return lax.dot_general(a, b, (((1,), (1,)), ((), ())), preferred_element_type=jnp.float32)


def halves(x):
    high = x.astype(jnp.bfloat16)
    return high, (x - high.astype(jnp.float32)).astype(jnp.bfloat16)


def table_times(high_ref, low_ref, x):
    if x.dtype == jnp.bfloat16:
        return dot(high_ref[...], x) + dot(low_ref[...], x)
    high, low = halves(x)
    return dot(high_ref[...], high) + dot(low_ref[...], high) + dot(high_ref[...], low)


def pick(rows_ref, row, step, count):
    return jnp.concatenate(
        [rows_ref[h, pl.ds(row, count, stride=step), :] for h in range(rows_ref.shape[0])], axis=1
    )


def place(rows_ref, row, step, value):
    for h in range(rows_ref.shape[0]):
        rows_ref[h, pl.ds(row, value.shape[0], stride=step), :] = value[:, h * 128 : (h + 1) * 128]


def fill(rows_ref, blocks):
    flat = blocks.reshape(rows_ref.shape[1], -1).astype(jnp.float32)
    for h in range(rows_ref.shape[0]):
        rows_ref[h] = flat[:, h * 128 : (h + 1) * 128]


def emptied(rows_ref, out_ref):
    flat = jnp.concatenate([rows_ref[h].astype(jnp.bfloat16) for h in range(rows_ref.shape[0])], axis=1)
    out_ref[...] = flat.reshape(out_ref.shape)


EARLY = (6, 5, 7)
LATE = (2, 3, 1, 4, 0)
NEIGHBOURS, REST = (3, 1), (2, 4, 0)


def fetch(held, order, refl_ref, held_ref, sems):
    share = held_ref.shape[2] // len(held)
    copies = {}
    for k in order + tuple(k for k in held if k not in order):
        i = held.index(k)
        start = pl.multiple_of((lax.axis_index("panel") ^ k) * share, share)
        copies[k] = pltpu.make_async_copy(
            refl_ref.at[:, :, pl.ds(start, share)], held_ref.at[:, :, pl.ds(i * share, share)], sems.at[i]
        )
        copies[k].start()
    return copies


def image_kernel(order, held, spread, first, keep, bands_ref, *refs):
    if spread:
        refl_ref, *refs = refs
    else:
        crossed, refl_ref, *refs = refs
        direct = bands_ref
    out_refs, refs = refs[: len(order)], refs[len(order) :]
    if spread:
        direct, crossed, *refs = refs
    held_ref, copies = refl_ref, {}
    if first:
        *refs, held_ref, sems = refs if keep is False else (*refs[1:-1], refs[0], refs[-1])
        copies = fetch(held, order, refl_ref, held_ref, sems)

    _, freqs, height, _ = held_ref.shape
    step = 2 * freqs
    groups, block, share = out_refs[0].shape
    count = groups * block // step
    if spread:
        rows = refs[0]
        fill(rows, bands_ref[...])
        for j in range(freqs):
            real, imag = pick(rows, 2 * j, step, count), pick(rows, 2 * j + 1, step, count)
            direct[j] = jnp.concatenate([real, imag], axis=0).astype(jnp.bfloat16)
            crossed[j] = jnp.concatenate([-imag, real], axis=0).astype(jnp.bfloat16)

    for k, out_ref in zip(order, out_refs, strict=True):
        if first:
            copies.pop(k).wait()
        i = held.index(k)
        at = slice(i * share, (i + 1) * share)
        images = [
            dot_nt(direct[j], held_ref[0, j, at]) + dot_nt(crossed[j], held_ref[1, j, at]) for j in range(freqs)
        ]
        images = jnp.stack(images).reshape(step, count, share)
        out_ref[...] = jnp.swapaxes(images, 0, 1).astype(jnp.bfloat16).reshape(groups, block, share)
    for copy in copies.values():
        copy.wait()


IN_VMEM = pl.BlockSpec(memory_space=pltpu.VMEM)


def call(kernel, name, out_shape, args, scratch=(), specs=None, flops=0):
    size = sum(a.size * a.dtype.itemsize for a in args)
    return pl.pallas_call(
        kernel,
        in_specs=specs or [IN_VMEM] * len(args),
        out_specs=jax.tree.map(lambda _: IN_VMEM, out_shape),
        out_shape=out_shape,
        scratch_shapes=list(scratch),
        compiler_params=pltpu.CompilerParams(vmem_limit_bytes=16 * MIB),
        cost_estimate=pl.CostEstimate(flops=flops, bytes_accessed=2 * size, transcendentals=0),
        name=name,
    )(*args)


def image_blocks(order, held, sources, reflection, panels, first, keep=True):
    spread = len(sources) == 1
    _, freqs, receivers, width = reflection.shape
    share = receivers // (panels if first else len(held))
    if spread:
        groups, height, _ = sources[0].shape
        count = groups * height // (2 * freqs)
        by_freq = jax.ShapeDtypeStruct((freqs, 2 * count, width), jnp.bfloat16)
    else:
        count = sources[0].shape[1] // 2
        height = 2 * freqs * count // lax.axis_size("freq")
        groups = lax.axis_size("freq")
    out_shape = [jax.ShapeDtypeStruct((groups, height, share), jnp.bfloat16)] * len(order)
    scratch = []
    if spread:
        out_shape += [by_freq, by_freq]
        scratch.append(pltpu.VMEM((width // 128, groups * height, 128), jnp.float32))
    specs = None
    if first:
        (out_shape if keep else scratch).append(pltpu.VMEM((2, freqs, share * len(held), width), reflection.dtype))
        scratch.append(pltpu.SemaphoreType.DMA((len(held),)))
        specs = [IN_VMEM] * len(sources) + [pl.BlockSpec(memory_space=pltpu.HBM)]
        reflection = pltpu.with_memory_space_constraint(reflection, pltpu.HBM)
    outs = call(
        lambda *refs: image_kernel(order, held, spread, first, keep, *refs),
        "image_blocks",
        out_shape,
        (*sources, reflection),
        scratch,
        specs,
        flops=4 * 2 * freqs * share * len(order) * width * count,
    )
    blocks, outs = outs[: len(order)], outs[len(order) :]
    return blocks, outs[:2] if spread else sources, outs[-1] if first and keep else reflection


def fetch_kernel(refl_ref, _, held_ref, sems):
    for copy in fetch(EARLY, EARLY, refl_ref, held_ref, sems).values():
        copy.wait()


def fetch_early(reflection, panels, after):
    parts, freqs, receivers, width = reflection.shape
    return call(
        fetch_kernel,
        "fetch_early",
        pltpu.VMEM((parts, freqs, receivers // panels * len(EARLY), width), reflection.dtype),
        (pltpu.with_memory_space_constraint(reflection, pltpu.HBM), after),
        [pltpu.SemaphoreType.DMA((len(EARLY),))],
        [pl.BlockSpec(memory_space=pltpu.HBM), pl.BlockSpec(memory_space=pl.ANY)],
    )


def return_kernel(panels, final, *refs):
    blocks, refl_ref, refs = refs[:panels], refs[panels], refs[panels + 1 :]
    groups, block, width = blocks[0].shape
    freqs = refl_ref.shape[1]
    step = 2 * freqs
    count = groups * block // step
    lanes = width // 128
    if final:
        before, *more, out_ref, rows, results = refs
    else:
        total_ref, rows = refs

    for p in range(panels):
        flat = blocks[p][...].reshape(groups * block, width).astype(jnp.float32)
        for h in range(lanes):
            rows[p * lanes + h] = flat[:, h * 128 : (h + 1) * 128]

    for j in range(freqs):
        total = before[j] if final else None
        for p in range(panels):
            of_panel = rows.at[pl.ds(p * lanes, lanes)]
            real = pick(of_panel, 2 * j, step, count)
            imag = pick(of_panel, 2 * j + 1, step, count)
            direct = jnp.concatenate([real, imag], axis=0).astype(jnp.bfloat16)
            crossed = jnp.concatenate([imag, -real], axis=0).astype(jnp.bfloat16)
            at = slice(p * width, (p + 1) * width)
            part = dot(direct, refl_ref[0, j, at]) + dot(crossed, refl_ref[1, j, at])
            total = part if total is None else total + part
        if final:
            place(results, 2 * j, step, total[:count])
            place(results, 2 * j + 1, step, total[count:])
        else:
            total_ref[j] = total
    if final:
        emptied(results, out_ref.at[:, :block])
        for ref in more:
            out_ref[:, block:] = ref[...].reshape(groups, -1, width)


def return_blocks(blocks, reflection, before=None, traces=()):
    panels = len(blocks)
    groups, height, width = blocks[0].shape
    _, freqs, _, sources = reflection.shape
    count = groups * height // (2 * freqs)
    final = before is not None
    more = sum(t.size // (groups * width) for t in traces)
    scratch = [pltpu.VMEM((panels * width // 128, groups * height, 128), jnp.float32)]
    if final:
        out_shape = jax.ShapeDtypeStruct((groups, height + more, sources), jnp.bfloat16)
        scratch.append(pltpu.VMEM((sources // 128, groups * height, 128), jnp.float32))
    else:
        out_shape = jax.ShapeDtypeStruct((freqs, 2 * count, sources), jnp.float32)
    return call(
        lambda *refs: return_kernel(panels, final, *refs),
        "return_blocks",
        out_shape,
        (*blocks, reflection, *([before] if final else []), *traces),
        scratch,
        flops=4 * reflection.size * count,
    )


def windowed(traces, onsets_ref, v):
    count = onsets_ref.shape[0] // lax.axis_size("freq")
    onsets = onsets_ref[pl.ds(lax.axis_index("freq") * count + v, 1), :]
    samples = lax.broadcasted_iota(jnp.int32, traces.shape, 0)
    return jnp.where((samples < onsets) | (samples > NT - onsets), traces, 0.0)


def start_kernel(high, low, traces_ref, first_ref, out_ref):
    blocks, count, share, width = traces_ref.shape
    rows = out_ref.shape[1] // count
    for v in range(count):
        spectra = table_times(high, low, traces_ref[:, v].reshape(blocks * share, width))
        first_ref[v] = spectra
        out_ref[:, v * rows : (v + 1) * rows] = spectra.astype(jnp.bfloat16).reshape(blocks, rows, width)


def start_bands(traces, forward, rows):
    blocks, count, _, width = traces.shape
    return call(
        start_kernel,
        "start_bands",
        [
            pltpu.VMEM((count, blocks * rows, width), jnp.float32),
            jax.ShapeDtypeStruct((blocks, count * rows, width), jnp.bfloat16),
        ],
        (*forward, traces),
    )


def upgoing_kernel(rows, ih, il, fh, fl, onsets_ref, images_ref, out_ref, *traces_ref):
    groups, height, width = images_ref.shape
    for v in range(height // rows):
        at = slice(v * rows, (v + 1) * rows)
        images = images_ref[:, at].reshape(groups * rows, width)
        traces = windowed(table_times(ih, il, images), onsets_ref, v)
        out_ref[:, at] = table_times(fh, fl, traces).astype(jnp.bfloat16).reshape(groups, rows, width)
        for ref in traces_ref:
            ref[:, v] = traces.astype(jnp.bfloat16).reshape(groups, -1, width)


def upgoing_blocks(images, onsets, tables, rows, with_traces):
    groups, height, width = images.shape
    out_shape = [jax.ShapeDtypeStruct(images.shape, jnp.bfloat16)]
    if with_traces:
        out_shape.append(jax.ShapeDtypeStruct((groups, height // rows, NT // groups, width), jnp.bfloat16))
    return call(
        lambda *refs: upgoing_kernel(rows, *refs), "upgoing_blocks", out_shape, (*tables, onsets, images)
    )


def focus_kernel(rows, ih, il, fh, fl, onsets_ref, first_ref, returns_ref, out_ref):
    groups, height, width = returns_ref.shape
    for v in range(height // rows):
        at = slice(v * rows, (v + 1) * rows)
        returns = returns_ref[:, at].reshape(groups * rows, width)
        traces = windowed(table_times(ih, il, returns), onsets_ref, v)
        spectra = first_ref[v] + table_times(fh, fl, traces)
        out_ref[:, at] = spectra.astype(jnp.bfloat16).reshape(groups, rows, width)


def focus_blocks(returns, first, onsets, tables, rows):
    return call(
        lambda *refs: focus_kernel(rows, *refs),
        "focus_blocks",
        jax.ShapeDtypeStruct(returns.shape, jnp.bfloat16),
        (*tables, onsets, first, returns),
    )


def trace_kernel(rows, ih, il, onsets_ref, returns_ref, out_ref):
    groups, count, _, width = out_ref.shape
    for v in range(count):
        returns = returns_ref[:, v * rows : (v + 1) * rows].reshape(groups * rows, width)
        traces = windowed(table_times(ih, il, returns), onsets_ref, v)
        out_ref[:, v] = traces.astype(jnp.bfloat16).reshape(groups, -1, width)


def trace_blocks(returns, onsets, inverse, rows, count):
    groups, _, width = returns.shape
    return call(
        lambda *refs: trace_kernel(rows, *refs),
        "trace_blocks",
        jax.ShapeDtypeStruct((groups, count, NT // groups, width), jnp.bfloat16),
        (*inverse, onsets, returns),
    )


def exchange(blocks, axis):
    return lax.all_to_all(blocks, axis, split_axis=0, concat_axis=0, tiled=True)


def send(block, k):
    return lax.ppermute(block, "panel", [(i, i ^ k) for i in range(lax.axis_size("panel"))])


def added(*blocks):
    total = blocks[0].astype(jnp.float32)
    for block in blocks[1:]:
        total = total + block.astype(jnp.float32)
    return total.astype(jnp.bfloat16)


def local(reflection, focus_init, onsets):
    groups = lax.axis_size("freq")
    panels = lax.axis_size("panel")
    freqs = reflection.shape[1]
    share, sources, width = focus_init.shape
    count = sources // groups
    rows = 2 * freqs
    forward, inverse = [[jnp.asarray(t) for t in pair] for pair in band_tables(freqs * groups, NT)]
    tables = inverse + forward

    def in_time(samples):
        samples = samples.reshape(groups, count, share, width)
        return jnp.transpose(samples, (2, 0, 1, 3)).reshape(share, sources, width).astype(jnp.float32)

    sent = focus_init.astype(jnp.bfloat16).reshape(share, groups, count, width).transpose(1, 2, 0, 3)
    first, blocks = start_bands(exchange(sent, "freq"), forward, rows)
    early = late = reflection
    for iteration in range(ITERS):
        is_first, last = iteration == 0, iteration == ITERS - 1
        bands = exchange(blocks, "freq")
        (b6, b5, b7), by_freq, early = image_blocks(EARLY, EARLY, (bands,), early, panels, is_first)
        r5, r7, r6 = send(b5, 1), send(b7, 3), send(b6, 4)
        near = NEIGHBOURS if is_first else LATE
        (b3, b1), _, _ = image_blocks(NEIGHBOURS, near, tuple(by_freq), late, panels, is_first, keep=False)
        s1, s3 = send(b1, 1), send(b3, 3)
        (b2, b4, b0), _, late = image_blocks(REST, LATE, tuple(by_freq), late, panels, is_first)
        s2, s4 = send(added(b2, r6), 2), send(added(b4, r5, r7), 4)
        images = exchange(added(b0, s1, s3, s2, s4), "freq")
        spectra, *traces = upgoing_blocks(images, onsets, tables, rows, last)
        m0 = exchange(spectra, "freq")
        m2, m4, m1, m3 = send(m0, 2), send(m0, 4), send(m0, 1), send(m0, 3)
        m6, m5, m7 = send(m2, 4), send(m4, 1), send(m4, 3)
        partial = return_blocks((m2, m3, m1, m4, m0), late)
        if last:
            partial, upgoing = lax.optimization_barrier((partial, exchange(traces[0], "freq")))
            early = fetch_early(reflection, panels, upgoing)
        returns = exchange(return_blocks((m6, m5, m7), early, partial), "freq")
        if last:
            upgoing = in_time(upgoing)
            traces = trace_blocks(returns, onsets, inverse, rows, count)
            focusing = focus_init + in_time(exchange(traces, "freq"))
        else:
            blocks = focus_blocks(returns, first, onsets, tables, rows)
    return (focusing, upgoing)


def solution(mesh):
    placed = (P(None, "freq", None, "panel"), P("freq", None, "panel"), P(None, "panel"))
    return jax.shard_map(
        local,
        mesh=mesh,
        in_specs=placed,
        out_specs=(P("freq", None, "panel"), P("freq", None, "panel")),
        check_vma=False,
    )
```

```python
import math

import jax
import jax.numpy as jnp
import ml_dtypes
import numpy as np
from jax import lax
from jax.experimental import pallas as pl
from jax.experimental.pallas import tpu as pltpu
from jax.sharding import PartitionSpec as P

NT = 512
ITERS = 2
MIB = 1024 * 1024


def split_table(table):
    high = table.astype(ml_dtypes.bfloat16)
    low = (table - high.astype(np.float32)).astype(ml_dtypes.bfloat16)
    return high, low


def band_tables(freq_count, time_count):
    harmonic = np.arange(1, freq_count + 1)
    phases = harmonic[:, None] * np.arange(time_count)[None, :] % time_count
    angles = phases * (2.0 * math.pi / time_count)
    factor = 1.0 / math.sqrt(time_count)
    cosines = np.stack([np.cos(angles), -np.sin(angles)], axis=1).reshape(2 * freq_count, time_count)
    forward = (cosines * factor).astype(np.float32)
    inverse = (cosines.T * (2.0 * factor)).astype(np.float32)
    return split_table(forward), split_table(inverse)


def dot(a, b):
    return jnp.dot(a, b, preferred_element_type=jnp.float32)


def dot_nt(a, b):
    return lax.dot_general(a, b, (((1,), (1,)), ((), ())), preferred_element_type=jnp.float32)


def halves(x):
    high = x.astype(jnp.bfloat16)
    return high, (x - high.astype(jnp.float32)).astype(jnp.bfloat16)


def table_times(high_ref, low_ref, x):
    if x.dtype == jnp.bfloat16:
        return dot(high_ref[...], x) + dot(low_ref[...], x)
    high, low = halves(x)
    return dot(high_ref[...], high) + dot(low_ref[...], high) + dot(high_ref[...], low)


def pick(rows_ref, row, step, count):
    return jnp.concatenate(
        [rows_ref[h, pl.ds(row, count, stride=step), :] for h in range(rows_ref.shape[0])], axis=1
    )


def place(rows_ref, row, step, value):
    for h in range(rows_ref.shape[0]):
        rows_ref[h, pl.ds(row, value.shape[0], stride=step), :] = value[:, h * 128 : (h + 1) * 128]


def fill(rows_ref, blocks):
    flat = blocks.reshape(rows_ref.shape[1], -1).astype(jnp.float32)
    for h in range(rows_ref.shape[0]):
        rows_ref[h] = flat[:, h * 128 : (h + 1) * 128]


def emptied(rows_ref, out_ref):
    flat = jnp.concatenate([rows_ref[h].astype(jnp.bfloat16) for h in range(rows_ref.shape[0])], axis=1)
    out_ref[...] = flat.reshape(out_ref.shape)


EARLY = (5, 7)
LATE = (2, 3, 1, 4, 0, 6)
NEIGHBOURS, REST, LAST = (6, 3, 1), (2, 4, 0), (6, 5, 7)


def fetch(held, order, refl_ref, held_ref, sems):
    share = held_ref.shape[2] // len(held)
    copies = {}
    for k in order + tuple(k for k in held if k not in order):
        i = held.index(k)
        start = pl.multiple_of((lax.axis_index("panel") ^ k) * share, share)
        copies[k] = pltpu.make_async_copy(
            refl_ref.at[:, :, pl.ds(start, share)], held_ref.at[:, :, pl.ds(i * share, share)], sems.at[i]
        )
        copies[k].start()
    return copies


def image_kernel(order, held, spread, first, keep, bands_ref, *refs):
    if spread:
        refl_ref, *refs = refs
    else:
        crossed, refl_ref, *refs = refs
        direct = bands_ref
    out_refs, refs = refs[: len(order)], refs[len(order) :]
    if spread:
        direct, crossed, *refs = refs
    held_ref, copies = refl_ref, {}
    if first:
        *refs, held_ref, sems = refs if keep is False else (*refs[1:-1], refs[0], refs[-1])
        copies = fetch(held, order, refl_ref, held_ref, sems)

    _, freqs, height, _ = held_ref.shape
    step = 2 * freqs
    groups, block, share = out_refs[0].shape
    count = groups * block // step
    if spread:
        rows = refs[0]
        fill(rows, bands_ref[...])
        for j in range(freqs):
            real, imag = pick(rows, 2 * j, step, count), pick(rows, 2 * j + 1, step, count)
            direct[j] = jnp.concatenate([real, imag], axis=0).astype(jnp.bfloat16)
            crossed[j] = jnp.concatenate([-imag, real], axis=0).astype(jnp.bfloat16)

    for k, out_ref in zip(order, out_refs, strict=True):
        if first:
            copies.pop(k).wait()
        i = held.index(k)
        at = slice(i * share, (i + 1) * share)
        images = [
            dot_nt(direct[j], held_ref[0, j, at]) + dot_nt(crossed[j], held_ref[1, j, at]) for j in range(freqs)
        ]
        images = jnp.stack(images).reshape(step, count, share)
        out_ref[...] = jnp.swapaxes(images, 0, 1).astype(jnp.bfloat16).reshape(groups, block, share)
    for copy in copies.values():
        copy.wait()


IN_VMEM = pl.BlockSpec(memory_space=pltpu.VMEM)


def call(kernel, name, out_shape, args, scratch=(), specs=None, flops=0):
    size = sum(a.size * a.dtype.itemsize for a in args)
    return pl.pallas_call(
        kernel,
        in_specs=specs or [IN_VMEM] * len(args),
        out_specs=jax.tree.map(lambda _: IN_VMEM, out_shape),
        out_shape=out_shape,
        scratch_shapes=list(scratch),
        compiler_params=pltpu.CompilerParams(vmem_limit_bytes=16 * MIB),
        cost_estimate=pl.CostEstimate(flops=flops, bytes_accessed=2 * size, transcendentals=0),
        name=name,
    )(*args)


def image_blocks(order, held, sources, reflection, panels, first, keep=True):
    spread = len(sources) == 1
    _, freqs, receivers, width = reflection.shape
    share = receivers // (panels if first else len(held))
    if spread:
        groups, height, _ = sources[0].shape
        count = groups * height // (2 * freqs)
        by_freq = jax.ShapeDtypeStruct((freqs, 2 * count, width), jnp.bfloat16)
    else:
        count = sources[0].shape[1] // 2
        height = 2 * freqs * count // lax.axis_size("freq")
        groups = lax.axis_size("freq")
    out_shape = [jax.ShapeDtypeStruct((groups, height, share), jnp.bfloat16)] * len(order)
    scratch = []
    if spread:
        out_shape += [by_freq, by_freq]
        scratch.append(pltpu.VMEM((width // 128, groups * height, 128), jnp.float32))
    specs = None
    if first:
        (out_shape if keep else scratch).append(pltpu.VMEM((2, freqs, share * len(held), width), reflection.dtype))
        scratch.append(pltpu.SemaphoreType.DMA((len(held),)))
        specs = [IN_VMEM] * len(sources) + [pl.BlockSpec(memory_space=pltpu.HBM)]
        reflection = pltpu.with_memory_space_constraint(reflection, pltpu.HBM)
    outs = call(
        lambda *refs: image_kernel(order, held, spread, first, keep, *refs),
        "image_blocks",
        out_shape,
        (*sources, reflection),
        scratch,
        specs,
        flops=4 * 2 * freqs * share * len(order) * width * count,
    )
    blocks, outs = outs[: len(order)], outs[len(order) :]
    return blocks, outs[:2] if spread else sources, outs[-1] if first and keep else reflection


def fetch_kernel(refl_ref, _, held_ref, sems):
    for copy in fetch(LAST, LAST, refl_ref, held_ref, sems).values():
        copy.wait()


def fetch_last(reflection, panels, after):
    parts, freqs, receivers, width = reflection.shape
    return call(
        fetch_kernel,
        "fetch_last",
        pltpu.VMEM((parts, freqs, receivers // panels * len(LAST), width), reflection.dtype),
        (pltpu.with_memory_space_constraint(reflection, pltpu.HBM), after),
        [pltpu.SemaphoreType.DMA((len(LAST),))],
        [pl.BlockSpec(memory_space=pltpu.HBM), pl.BlockSpec(memory_space=pl.ANY)],
    )


def return_kernel(panels, final, order, *refs):
    blocks, refl_ref, refs = refs[:panels], refs[panels], refs[panels + 1 :]
    groups, block, width = blocks[0].shape
    freqs = refl_ref.shape[1]
    step = 2 * freqs
    count = groups * block // step
    lanes = width // 128
    if final:
        before, out_ref, rows, results = refs
    else:
        total_ref, rows, *refs = refs
    if order:
        held_ref, sems = refs
        copies = fetch(order, order, refl_ref, held_ref, sems)
        refl_ref = held_ref

    for p in range(panels):
        flat = blocks[p][...].reshape(groups * block, width).astype(jnp.float32)
        for h in range(lanes):
            rows[p * lanes + h] = flat[:, h * 128 : (h + 1) * 128]

    def product(j, p):
        of_panel = rows.at[pl.ds(p * lanes, lanes)]
        real = pick(of_panel, 2 * j, step, count)
        imag = pick(of_panel, 2 * j + 1, step, count)
        direct = jnp.concatenate([real, imag], axis=0).astype(jnp.bfloat16)
        crossed = jnp.concatenate([imag, -real], axis=0).astype(jnp.bfloat16)
        at = slice(p * width, (p + 1) * width)
        return dot(direct, refl_ref[0, j, at]) + dot(crossed, refl_ref[1, j, at])

    for p, k in enumerate(order):
        copies[k].wait()
        for j in range(freqs):
            total_ref[j] = product(j, p) if p == 0 else total_ref[j] + product(j, p)
    if order:
        return

    for j in range(freqs):
        total = before[j] if final else None
        for p in range(panels):
            part = product(j, p)
            total = part if total is None else total + part
        if final:
            place(results, 2 * j, step, total[:count])
            place(results, 2 * j + 1, step, total[count:])
        else:
            total_ref[j] = total
    if final:
        emptied(results, out_ref)


def return_blocks(blocks, reflection, before=None, order=()):
    panels = len(blocks)
    groups, height, width = blocks[0].shape
    _, freqs, _, sources = reflection.shape
    count = groups * height // (2 * freqs)
    final = before is not None
    scratch = [pltpu.VMEM((panels * width // 128, groups * height, 128), jnp.float32)]
    specs = None
    if final:
        out_shape = jax.ShapeDtypeStruct((groups, height, sources), jnp.bfloat16)
        scratch.append(pltpu.VMEM((sources // 128, groups * height, 128), jnp.float32))
    else:
        out_shape = jax.ShapeDtypeStruct((freqs, 2 * count, sources), jnp.float32)
    if order:
        scratch.append(pltpu.VMEM((2, freqs, width * panels, sources), reflection.dtype))
        scratch.append(pltpu.SemaphoreType.DMA((panels,)))
        specs = [IN_VMEM] * panels + [pl.BlockSpec(memory_space=pltpu.HBM)]
        reflection = pltpu.with_memory_space_constraint(reflection, pltpu.HBM)
    return call(
        lambda *refs: return_kernel(panels, final, order, *refs),
        "return_blocks",
        out_shape,
        (*blocks, reflection, *([before] if final else [])),
        scratch,
        specs,
        flops=4 * 2 * freqs * width * panels * sources * count,
    )


def windowed(traces, onsets_ref, v):
    count = onsets_ref.shape[0] // lax.axis_size("freq")
    onsets = onsets_ref[pl.ds(lax.axis_index("freq") * count + v, 1), :]
    samples = lax.broadcasted_iota(jnp.int32, traces.shape, 0)
    return jnp.where((samples < onsets) | (samples > NT - onsets), traces, 0.0)


def start_kernel(high, low, traces_ref, first_ref, out_ref):
    blocks, count, share, width = traces_ref.shape
    rows = out_ref.shape[1] // count
    for v in range(count):
        spectra = table_times(high, low, traces_ref[:, v].reshape(blocks * share, width))
        first_ref[v] = spectra
        out_ref[:, v * rows : (v + 1) * rows] = spectra.astype(jnp.bfloat16).reshape(blocks, rows, width)


def start_bands(traces, forward, rows):
    blocks, count, _, width = traces.shape
    return call(
        start_kernel,
        "start_bands",
        [
            pltpu.VMEM((count, blocks * rows, width), jnp.float32),
            jax.ShapeDtypeStruct((blocks, count * rows, width), jnp.bfloat16),
        ],
        (*forward, traces),
    )


def upgoing_kernel(rows, ih, il, fh, fl, onsets_ref, images_ref, out_ref, *traces_ref):
    groups, height, width = images_ref.shape
    for v in range(height // rows):
        at = slice(v * rows, (v + 1) * rows)
        images = images_ref[:, at].reshape(groups * rows, width)
        traces = windowed(table_times(ih, il, images), onsets_ref, v)
        out_ref[:, at] = table_times(fh, fl, traces).astype(jnp.bfloat16).reshape(groups, rows, width)
        for ref in traces_ref:
            ref[:, v] = traces.astype(jnp.bfloat16).reshape(groups, -1, width)


def upgoing_blocks(images, onsets, tables, rows, with_traces):
    groups, height, width = images.shape
    out_shape = [jax.ShapeDtypeStruct(images.shape, jnp.bfloat16)]
    if with_traces:
        out_shape.append(jax.ShapeDtypeStruct((groups, height // rows, NT // groups, width), jnp.bfloat16))
    return call(
        lambda *refs: upgoing_kernel(rows, *refs), "upgoing_blocks", out_shape, (*tables, onsets, images)
    )


def focus_kernel(rows, ih, il, fh, fl, onsets_ref, first_ref, returns_ref, out_ref):
    groups, height, width = returns_ref.shape
    for v in range(height // rows):
        at = slice(v * rows, (v + 1) * rows)
        returns = returns_ref[:, at].reshape(groups * rows, width)
        traces = windowed(table_times(ih, il, returns), onsets_ref, v)
        spectra = first_ref[v] + table_times(fh, fl, traces)
        out_ref[:, at] = spectra.astype(jnp.bfloat16).reshape(groups, rows, width)


def focus_blocks(returns, first, onsets, tables, rows):
    return call(
        lambda *refs: focus_kernel(rows, *refs),
        "focus_blocks",
        jax.ShapeDtypeStruct(returns.shape, jnp.bfloat16),
        (*tables, onsets, first, returns),
    )


def trace_kernel(rows, ih, il, onsets_ref, returns_ref, out_ref):
    groups, count, _, width = out_ref.shape
    for v in range(count):
        returns = returns_ref[:, v * rows : (v + 1) * rows].reshape(groups * rows, width)
        traces = windowed(table_times(ih, il, returns), onsets_ref, v)
        out_ref[:, v] = traces.astype(jnp.bfloat16).reshape(groups, -1, width)


def trace_blocks(returns, onsets, inverse, rows, count):
    groups, _, width = returns.shape
    return call(
        lambda *refs: trace_kernel(rows, *refs),
        "trace_blocks",
        jax.ShapeDtypeStruct((groups, count, NT // groups, width), jnp.bfloat16),
        (*inverse, onsets, returns),
    )


def exchange(blocks, axis):
    return lax.all_to_all(blocks, axis, split_axis=0, concat_axis=0, tiled=True)


def send(block, k):
    return lax.ppermute(block, "panel", [(i, i ^ k) for i in range(lax.axis_size("panel"))])


def added(*blocks):
    total = blocks[0].astype(jnp.float32)
    for block in blocks[1:]:
        total = total + block.astype(jnp.float32)
    return total.astype(jnp.bfloat16)


def local(reflection, focus_init, onsets):
    groups = lax.axis_size("freq")
    panels = lax.axis_size("panel")
    freqs = reflection.shape[1]
    share, sources, width = focus_init.shape
    count = sources // groups
    rows = 2 * freqs
    forward, inverse = [[jnp.asarray(t) for t in pair] for pair in band_tables(freqs * groups, NT)]
    tables = inverse + forward

    def in_time(samples):
        samples = samples.reshape(groups, count, share, width)
        return jnp.transpose(samples, (2, 0, 1, 3)).reshape(share, sources, width).astype(jnp.float32)

    sent = focus_init.astype(jnp.bfloat16).reshape(share, groups, count, width).transpose(1, 2, 0, 3)
    first, blocks = start_bands(exchange(sent, "freq"), forward, rows)
    early = late = reflection
    for iteration in range(ITERS):
        is_first, last = iteration == 0, iteration == ITERS - 1
        bands = exchange(blocks, "freq")
        (b5, b7), by_freq, early = image_blocks(EARLY, EARLY, (bands,), early, panels, is_first)
        r5, r7 = send(b5, 1), send(b7, 3)
        near = NEIGHBOURS if is_first else LATE
        (b6, b3, b1), _, _ = image_blocks(NEIGHBOURS, near, tuple(by_freq), late, panels, is_first, keep=False)
        r6, s1, s3 = send(b6, 4), send(b1, 1), send(b3, 3)
        (b2, b4, b0), _, late = image_blocks(REST, LATE, tuple(by_freq), late, panels, is_first)
        s2, s4 = send(added(b2, r6), 2), send(added(b4, r5, r7), 4)
        images = exchange(added(b0, s1, s3, s2, s4), "freq")
        spectra, *traces = upgoing_blocks(images, onsets, tables, rows, last)
        m0 = exchange(spectra, "freq")
        m2, m4, m1, m3 = send(m0, 2), send(m0, 4), send(m0, 1), send(m0, 3)
        m6, m5, m7 = send(m2, 4), send(m4, 1), send(m4, 3)
        if last:
            partial = return_blocks((m2, m3, m1, m4, m0), reflection, order=LATE[:5])
            partial, upgoing = lax.optimization_barrier((partial, exchange(traces[0], "freq")))
            returns = return_blocks((m6, m5, m7), fetch_last(reflection, panels, upgoing), partial)
        else:
            partial = return_blocks((m2, m3, m1, m4, m0, m6), late)
            returns = return_blocks((m5, m7), early, partial)
        returns = exchange(returns, "freq")
        if last:
            upgoing = in_time(upgoing)
            traces = trace_blocks(returns, onsets, inverse, rows, count)
            focusing = focus_init + in_time(exchange(traces, "freq"))
        else:
            blocks = focus_blocks(returns, first, onsets, tables, rows)
    return (focusing, upgoing)


def solution(mesh):
    placed = (P(None, "freq", None, "panel"), P("freq", None, "panel"), P(None, "panel"))
    return jax.shard_map(
        local,
        mesh=mesh,
        in_specs=placed,
        out_specs=(P("freq", None, "panel"), P("freq", None, "panel")),
        check_vma=False,
    )
```

```python
import math

import jax
import jax.numpy as jnp
import ml_dtypes
import numpy as np
from jax import lax
from jax.experimental import pallas as pl
from jax.experimental.pallas import tpu as pltpu
from jax.sharding import PartitionSpec as P

NT = 512
ITERS = 2
MIB = 1024 * 1024


def split_table(table):
    high = table.astype(ml_dtypes.bfloat16)
    low = (table - high.astype(np.float32)).astype(ml_dtypes.bfloat16)
    return high, low


def band_tables(freq_count, time_count):
    harmonic = np.arange(1, freq_count + 1)
    phases = harmonic[:, None] * np.arange(time_count)[None, :] % time_count
    angles = phases * (2.0 * math.pi / time_count)
    factor = 1.0 / math.sqrt(time_count)
    cosines = np.stack([np.cos(angles), -np.sin(angles)], axis=1).reshape(2 * freq_count, time_count)
    forward = (cosines * factor).astype(np.float32)
    inverse = (cosines.T * (2.0 * factor)).astype(np.float32)
    return split_table(forward), split_table(inverse)


def dot(a, b):
    return jnp.dot(a, b, preferred_element_type=jnp.float32)


def dot_nt(a, b):
    return lax.dot_general(a, b, (((1,), (1,)), ((), ())), preferred_element_type=jnp.float32)


def halves(x):
    high = x.astype(jnp.bfloat16)
    return high, (x - high.astype(jnp.float32)).astype(jnp.bfloat16)


def table_times(high_ref, low_ref, x):
    if x.dtype == jnp.bfloat16:
        return dot(high_ref[...], x) + dot(low_ref[...], x)
    high, low = halves(x)
    return dot(high_ref[...], high) + dot(low_ref[...], high) + dot(high_ref[...], low)


def pick(rows_ref, row, step, count):
    return jnp.concatenate(
        [rows_ref[h, pl.ds(row, count, stride=step), :] for h in range(rows_ref.shape[0])], axis=1
    )


def place(rows_ref, row, step, value):
    for h in range(rows_ref.shape[0]):
        rows_ref[h, pl.ds(row, value.shape[0], stride=step), :] = value[:, h * 128 : (h + 1) * 128]


def fill(rows_ref, blocks):
    flat = blocks.reshape(rows_ref.shape[1], -1).astype(jnp.float32)
    for h in range(rows_ref.shape[0]):
        rows_ref[h] = flat[:, h * 128 : (h + 1) * 128]


def emptied(rows_ref, out_ref):
    flat = jnp.concatenate([rows_ref[h].astype(jnp.bfloat16) for h in range(rows_ref.shape[0])], axis=1)
    out_ref[...] = flat.reshape(out_ref.shape)


EARLY = (5, 7)
LATE = (2, 3, 1, 4, 0, 6)
NEIGHBOURS, REST, LAST = (6, 3, 1), (2, 4, 0), (6, 5, 7)


def fetch(held, order, refl_ref, held_ref, sems):
    share = held_ref.shape[2] // len(held)
    copies = {}
    for k in order + tuple(k for k in held if k not in order):
        i = held.index(k)
        start = pl.multiple_of((lax.axis_index("panel") ^ k) * share, share)
        copies[k] = pltpu.make_async_copy(
            refl_ref.at[:, :, pl.ds(start, share)], held_ref.at[:, :, pl.ds(i * share, share)], sems.at[i]
        )
        copies[k].start()
    return copies


def image_kernel(order, held, spread, first, keep, bands_ref, *refs):
    if spread:
        refl_ref, *refs = refs
    else:
        crossed, refl_ref, *refs = refs
        direct = bands_ref
    out_refs, refs = refs[: len(order)], refs[len(order) :]
    if spread:
        direct, crossed, *refs = refs
    held_ref, copies = refl_ref, {}
    if first:
        *refs, held_ref, sems = refs if keep is False else (*refs[1:-1], refs[0], refs[-1])
        copies = fetch(held, order, refl_ref, held_ref, sems)

    _, freqs, height, _ = held_ref.shape
    step = 2 * freqs
    groups, block, share = out_refs[0].shape
    count = groups * block // step
    if spread:
        rows = refs[0]
        fill(rows, bands_ref[...])
        for j in range(freqs):
            real, imag = pick(rows, 2 * j, step, count), pick(rows, 2 * j + 1, step, count)
            direct[j] = jnp.concatenate([real, imag], axis=0).astype(jnp.bfloat16)
            crossed[j] = jnp.concatenate([-imag, real], axis=0).astype(jnp.bfloat16)

    for k, out_ref in zip(order, out_refs, strict=True):
        if first:
            copies.pop(k).wait()
        i = held.index(k)
        at = slice(i * share, (i + 1) * share)
        images = [
            dot_nt(direct[j], held_ref[0, j, at]) + dot_nt(crossed[j], held_ref[1, j, at]) for j in range(freqs)
        ]
        images = jnp.stack(images).reshape(step, count, share)
        out_ref[...] = jnp.swapaxes(images, 0, 1).astype(jnp.bfloat16).reshape(groups, block, share)
    for copy in copies.values():
        copy.wait()


IN_VMEM = pl.BlockSpec(memory_space=pltpu.VMEM)


def call(kernel, name, out_shape, args, scratch=(), specs=None, flops=0):
    size = sum(a.size * a.dtype.itemsize for a in args)
    return pl.pallas_call(
        kernel,
        in_specs=specs or [IN_VMEM] * len(args),
        out_specs=jax.tree.map(lambda _: IN_VMEM, out_shape),
        out_shape=out_shape,
        scratch_shapes=list(scratch),
        compiler_params=pltpu.CompilerParams(vmem_limit_bytes=16 * MIB),
        cost_estimate=pl.CostEstimate(flops=flops, bytes_accessed=2 * size, transcendentals=0),
        name=name,
    )(*args)


def image_blocks(order, held, sources, reflection, panels, first, keep=True):
    spread = len(sources) == 1
    _, freqs, receivers, width = reflection.shape
    share = receivers // (panels if first else len(held))
    if spread:
        groups, height, _ = sources[0].shape
        count = groups * height // (2 * freqs)
        by_freq = jax.ShapeDtypeStruct((freqs, 2 * count, width), jnp.bfloat16)
    else:
        count = sources[0].shape[1] // 2
        height = 2 * freqs * count // lax.axis_size("freq")
        groups = lax.axis_size("freq")
    out_shape = [jax.ShapeDtypeStruct((groups, height, share), jnp.bfloat16)] * len(order)
    scratch = []
    if spread:
        out_shape += [by_freq, by_freq]
        scratch.append(pltpu.VMEM((width // 128, groups * height, 128), jnp.float32))
    specs = None
    if first:
        (out_shape if keep else scratch).append(pltpu.VMEM((2, freqs, share * len(held), width), reflection.dtype))
        scratch.append(pltpu.SemaphoreType.DMA((len(held),)))
        specs = [IN_VMEM] * len(sources) + [pl.BlockSpec(memory_space=pltpu.HBM)]
        reflection = pltpu.with_memory_space_constraint(reflection, pltpu.HBM)
    outs = call(
        lambda *refs: image_kernel(order, held, spread, first, keep, *refs),
        "image_blocks",
        out_shape,
        (*sources, reflection),
        scratch,
        specs,
        flops=4 * 2 * freqs * share * len(order) * width * count,
    )
    blocks, outs = outs[: len(order)], outs[len(order) :]
    return blocks, outs[:2] if spread else sources, outs[-1] if first and keep else reflection


def fetch_kernel(refl_ref, _, held_ref, sems):
    for copy in fetch(LAST, LAST, refl_ref, held_ref, sems).values():
        copy.wait()


def fetch_last(reflection, panels, after):
    parts, freqs, receivers, width = reflection.shape
    return call(
        fetch_kernel,
        "fetch_last",
        pltpu.VMEM((parts, freqs, receivers // panels * len(LAST), width), reflection.dtype),
        (pltpu.with_memory_space_constraint(reflection, pltpu.HBM), after),
        [pltpu.SemaphoreType.DMA((len(LAST),))],
        [pl.BlockSpec(memory_space=pltpu.HBM), pl.BlockSpec(memory_space=pl.ANY)],
    )


def return_kernel(panels, final, order, *refs):
    blocks, refl_ref, refs = refs[:panels], refs[panels], refs[panels + 1 :]
    groups, block, width = blocks[0].shape
    freqs = refl_ref.shape[1]
    step = 2 * freqs
    count = groups * block // step
    lanes = width // 128
    if final:
        before, out_ref, rows, results = refs
    else:
        total_ref, rows, *refs = refs
    if order:
        held_ref, sems = refs
        copies = fetch(order, order, refl_ref, held_ref, sems)
        refl_ref = held_ref

    for p in range(panels):
        flat = blocks[p][...].reshape(groups * block, width).astype(jnp.float32)
        for h in range(lanes):
            rows[p * lanes + h] = flat[:, h * 128 : (h + 1) * 128]

    def product(j, p):
        of_panel = rows.at[pl.ds(p * lanes, lanes)]
        real = pick(of_panel, 2 * j, step, count)
        imag = pick(of_panel, 2 * j + 1, step, count)
        direct = jnp.concatenate([real, imag], axis=0).astype(jnp.bfloat16)
        crossed = jnp.concatenate([imag, -real], axis=0).astype(jnp.bfloat16)
        at = slice(p * width, (p + 1) * width)
        return dot(direct, refl_ref[0, j, at]) + dot(crossed, refl_ref[1, j, at])

    for p, k in enumerate(order):
        copies[k].wait()
        for j in range(freqs):
            total_ref[j] = product(j, p) if p == 0 else total_ref[j] + product(j, p)
    if order:
        return

    for j in range(freqs):
        total = before[j] if final else None
        for p in range(panels):
            part = product(j, p)
            total = part if total is None else total + part
        if final:
            place(results, 2 * j, step, total[:count])
            place(results, 2 * j + 1, step, total[count:])
        else:
            total_ref[j] = total
    if final:
        emptied(results, out_ref)


def return_blocks(blocks, reflection, before=None, order=()):
    panels = len(blocks)
    groups, height, width = blocks[0].shape
    _, freqs, _, sources = reflection.shape
    count = groups * height // (2 * freqs)
    final = before is not None
    scratch = [pltpu.VMEM((panels * width // 128, groups * height, 128), jnp.float32)]
    specs = None
    if final:
        out_shape = jax.ShapeDtypeStruct((groups, height, sources), jnp.bfloat16)
        scratch.append(pltpu.VMEM((sources // 128, groups * height, 128), jnp.float32))
    else:
        out_shape = jax.ShapeDtypeStruct((freqs, 2 * count, sources), jnp.float32)
    if order:
        scratch.append(pltpu.VMEM((2, freqs, width * panels, sources), reflection.dtype))
        scratch.append(pltpu.SemaphoreType.DMA((panels,)))
        specs = [IN_VMEM] * panels + [pl.BlockSpec(memory_space=pltpu.HBM)]
        reflection = pltpu.with_memory_space_constraint(reflection, pltpu.HBM)
    return call(
        lambda *refs: return_kernel(panels, final, order, *refs),
        "return_blocks",
        out_shape,
        (*blocks, reflection, *([before] if final else [])),
        scratch,
        specs,
        flops=4 * 2 * freqs * width * panels * sources * count,
    )


def windowed(traces, onsets_ref, v):
    count = onsets_ref.shape[0] // lax.axis_size("freq")
    onsets = onsets_ref[pl.ds(lax.axis_index("freq") * count + v, 1), :]
    samples = lax.broadcasted_iota(jnp.int32, traces.shape, 0)
    return jnp.where((samples < onsets) | (samples > NT - onsets), traces, 0.0)


def start_kernel(high, low, traces_ref, first_ref, out_ref):
    blocks, count, share, width = traces_ref.shape
    rows = out_ref.shape[1] // count
    for v in range(count):
        spectra = table_times(high, low, traces_ref[:, v].reshape(blocks * share, width))
        first_ref[v] = spectra
        out_ref[:, v * rows : (v + 1) * rows] = spectra.astype(jnp.bfloat16).reshape(blocks, rows, width)


def start_bands(traces, forward, rows):
    blocks, count, _, width = traces.shape
    return call(
        start_kernel,
        "start_bands",
        [
            pltpu.VMEM((count, blocks * rows, width), jnp.float32),
            jax.ShapeDtypeStruct((blocks, count * rows, width), jnp.bfloat16),
        ],
        (*forward, traces),
    )


def upgoing_kernel(rows, ih, il, fh, fl, onsets_ref, images_ref, out_ref, *traces_ref):
    groups, height, width = images_ref.shape
    for v in range(height // rows):
        at = slice(v * rows, (v + 1) * rows)
        images = images_ref[:, at].reshape(groups * rows, width)
        traces = windowed(table_times(ih, il, images), onsets_ref, v)
        out_ref[:, at] = table_times(fh, fl, traces).astype(jnp.bfloat16).reshape(groups, rows, width)
        for ref in traces_ref:
            ref[:, v] = traces.astype(jnp.bfloat16).reshape(groups, -1, width)


def upgoing_blocks(images, onsets, tables, rows, with_traces):
    groups, height, width = images.shape
    out_shape = [jax.ShapeDtypeStruct(images.shape, jnp.bfloat16)]
    if with_traces:
        out_shape.append(jax.ShapeDtypeStruct((groups, height // rows, NT // groups, width), jnp.bfloat16))
    return call(
        lambda *refs: upgoing_kernel(rows, *refs), "upgoing_blocks", out_shape, (*tables, onsets, images)
    )


def focus_kernel(rows, ih, il, fh, fl, onsets_ref, first_ref, returns_ref, out_ref):
    groups, height, width = returns_ref.shape
    for v in range(height // rows):
        at = slice(v * rows, (v + 1) * rows)
        returns = returns_ref[:, at].reshape(groups * rows, width)
        traces = windowed(table_times(ih, il, returns), onsets_ref, v)
        spectra = first_ref[v] + table_times(fh, fl, traces)
        out_ref[:, at] = spectra.astype(jnp.bfloat16).reshape(groups, rows, width)


def focus_blocks(returns, first, onsets, tables, rows):
    return call(
        lambda *refs: focus_kernel(rows, *refs),
        "focus_blocks",
        jax.ShapeDtypeStruct(returns.shape, jnp.bfloat16),
        (*tables, onsets, first, returns),
    )


def trace_kernel(rows, ih, il, onsets_ref, returns_ref, out_ref):
    groups, count, _, width = out_ref.shape
    for v in range(count):
        returns = returns_ref[:, v * rows : (v + 1) * rows].reshape(groups * rows, width)
        traces = windowed(table_times(ih, il, returns), onsets_ref, v)
        out_ref[:, v] = traces.astype(jnp.bfloat16).reshape(groups, -1, width)


def trace_blocks(returns, onsets, inverse, rows, count):
    groups, _, width = returns.shape
    return call(
        lambda *refs: trace_kernel(rows, *refs),
        "trace_blocks",
        jax.ShapeDtypeStruct((groups, count, NT // groups, width), jnp.bfloat16),
        (*inverse, onsets, returns),
    )


def sum_kernel(samples_ref, focus_ref, out_ref, sums, sems):
    groups, count, share, width = samples_ref.shape
    half = share // 2
    copies = []
    for i in range(2):
        at = slice(i * half, (i + 1) * half)
        samples = samples_ref[:, :, at].reshape(groups * count, half, width).astype(jnp.float32)
        sums[at] = focus_ref[at] + jnp.swapaxes(samples, 0, 1)
        copies.append(pltpu.make_async_copy(sums.at[at], out_ref.at[at], sems.at[i]))
        copies[-1].start()
    for copy in copies:
        copy.wait()


def focus_sum(samples, focus_init):
    size = 2 * focus_init.size * focus_init.dtype.itemsize
    return pl.pallas_call(
        sum_kernel,
        in_specs=[IN_VMEM, IN_VMEM],
        out_specs=pl.BlockSpec(memory_space=pltpu.HBM),
        out_shape=jax.ShapeDtypeStruct(focus_init.shape, focus_init.dtype),
        scratch_shapes=[pltpu.VMEM(focus_init.shape, focus_init.dtype), pltpu.SemaphoreType.DMA((2,))],
        compiler_params=pltpu.CompilerParams(vmem_limit_bytes=16 * MIB),
        cost_estimate=pl.CostEstimate(flops=focus_init.size, bytes_accessed=size, transcendentals=0),
        name="focus_sum",
    )(samples, focus_init)


def exchange(blocks, axis):
    return lax.all_to_all(blocks, axis, split_axis=0, concat_axis=0, tiled=True)


def send(block, k):
    return lax.ppermute(block, "panel", [(i, i ^ k) for i in range(lax.axis_size("panel"))])


def added(*blocks):
    total = blocks[0].astype(jnp.float32)
    for block in blocks[1:]:
        total = total + block.astype(jnp.float32)
    return total.astype(jnp.bfloat16)


def local(reflection, focus_init, onsets):
    groups = lax.axis_size("freq")
    panels = lax.axis_size("panel")
    freqs = reflection.shape[1]
    share, sources, width = focus_init.shape
    count = sources // groups
    rows = 2 * freqs
    forward, inverse = [[jnp.asarray(t) for t in pair] for pair in band_tables(freqs * groups, NT)]
    tables = inverse + forward

    def in_time(samples):
        samples = samples.reshape(groups, count, share, width)
        return jnp.transpose(samples, (2, 0, 1, 3)).reshape(share, sources, width).astype(jnp.float32)

    sent = focus_init.astype(jnp.bfloat16).reshape(share, groups, count, width).transpose(1, 2, 0, 3)
    first, blocks = start_bands(exchange(sent, "freq"), forward, rows)
    early = late = reflection
    for iteration in range(ITERS):
        is_first, last = iteration == 0, iteration == ITERS - 1
        bands = exchange(blocks, "freq")
        (b5, b7), by_freq, early = image_blocks(EARLY, EARLY, (bands,), early, panels, is_first)
        r5, r7 = send(b5, 1), send(b7, 3)
        near = NEIGHBOURS if is_first else LATE
        (b6, b3, b1), _, _ = image_blocks(NEIGHBOURS, near, tuple(by_freq), late, panels, is_first, keep=False)
        r6, s1, s3 = send(b6, 4), send(b1, 1), send(b3, 3)
        (b2, b4, b0), _, late = image_blocks(REST, LATE, tuple(by_freq), late, panels, is_first)
        s2, s4 = send(added(b2, r6), 2), send(added(b4, r5, r7), 4)
        images = exchange(added(b0, s1, s3, s2, s4), "freq")
        spectra, *traces = upgoing_blocks(images, onsets, tables, rows, last)
        m0 = exchange(spectra, "freq")
        m2, m4, m1, m3 = send(m0, 2), send(m0, 4), send(m0, 1), send(m0, 3)
        m6, m5, m7 = send(m2, 4), send(m4, 1), send(m4, 3)
        if last:
            partial = return_blocks((m2, m3, m1, m4, m0), reflection, order=LATE[:5])
            partial, upgoing = lax.optimization_barrier((partial, exchange(traces[0], "freq")))
            returns = return_blocks((m6, m5, m7), fetch_last(reflection, panels, upgoing), partial)
        else:
            partial = return_blocks((m2, m3, m1, m4, m0, m6), late)
            returns = return_blocks((m5, m7), early, partial)
        returns = exchange(returns, "freq")
        if last:
            upgoing = in_time(upgoing)
            traces = trace_blocks(returns, onsets, inverse, rows, count)
            focusing = focus_sum(exchange(traces, "freq"), focus_init)
        else:
            blocks = focus_blocks(returns, first, onsets, tables, rows)
    return (focusing, upgoing)


def solution(mesh):
    placed = (P(None, "freq", None, "panel"), P("freq", None, "panel"), P(None, "panel"))
    return jax.shard_map(
        local,
        mesh=mesh,
        in_specs=placed,
        out_specs=(P("freq", None, "panel"), P("freq", None, "panel")),
        check_vma=False,
    )
```
